256 devices in a mesh: dp: 16 (over z, core), expert: 16 (over x, y).
Axes of the slice: x: 4, y: 4, z: 8, core: 2. Of those that a mesh axis runs over, the one named last changes fastest.
Arguments:
- history: bfloat16 [512, 1024, 2048], P(('dp', 'expert')), may hold values from -6 to 6
- lengths: int32 [512], P(('dp', 'expert')), may hold values from 64 to 1024, as said below
- user_query: bfloat16 [512, 2048], P(('dp', 'expert')), may hold values from -1000 to 1000
- pos_item: bfloat16 [512, 2048], P(('dp', 'expert')), may hold values from -6 to 6
- neg_index: int32 [512, 63], P(('dp', 'expert')), may hold values from 0 to 511
- routes: int32 [32768, 2], P(('dp', 'expert')), may hold values from 0 to 15, all different within a row; in each aligned block of 128 rows (0 to 127, 128 to 255, ...) at most 32 rows name the same one
- w_router: bfloat16 [2048, 16], replicated, may hold values from -0.125 to 0.125
- w_gate: bfloat16 [16, 2048, 768], P('expert', 'dp'), may hold values from -0.125 to 0.125
- w_up: bfloat16 [16, 2048, 768], P('expert', 'dp'), may hold values from -0.125 to 0.125
- w_down: bfloat16 [16, 768, 2048], P('expert', None, 'dp'), may hold values from -0.21875 to 0.21875
- out_gain: float32 [2048], replicated, may hold values from 0.25 to 1.75
Outputs:
- losses: float32 [512], P(('dp', 'expert'))
- grad_gate: float32 [16, 2048, 768], P('expert', 'dp')
- grad_up: float32 [16, 2048, 768], P('expert', 'dp')
- grad_down: float32 [16, 768, 2048], P('expert', None, 'dp')
- grad_router: float32 [2048, 16], replicated
The draws below stay inside these ranges and needn't reach their ends.
Inputs may be any that keep to these rules, and one draw needn't show every extreme that they name: `lengths`: every device's block of 2 users holds one user with all 1024 events. `neg_index`: indices of users anywhere in the batch. `routes`: each row names two different experts; among the rows of one device no expert is named more than 32 times, a bound that some block reaches.
All inputs are finite; a program needn't handle non-finite values.
Results may differ from the reference program's by a relative error of at most 0.017.
Values may be sent and summed in bfloat16 or wider, within the bound.
A program may use at most 128 MiB of HBM per device.

```python
import math
import jax
import jax.numpy as jnp
import numpy as np
from jax import lax

D = 2048
HEADS = 16
HEAD = 128
FF = 768
EXPERTS = 16
CANDS = 64
NEG = 63
U_DEV = 2
HIST = 1024
CAP = 32
USERS = 512
ROWS = 32768
N_DP = 16
N_EXPERT = 16


def draw_lengths(key, part):
    key_len = jax.random.fold_in(key, 11)
    key_full = jax.random.fold_in(key, 12)
    low_bound = max(1, HIST // 16)
    drawn = jax.random.randint(key_len, (USERS,), low_bound, HIST + 1, dtype=jnp.int32)
    device_count = USERS // U_DEV
    chosen = jax.random.randint(key_full, (device_count,), 0, U_DEV, dtype=jnp.int32)
    full_rows = jnp.arange(device_count, dtype=jnp.int32) * U_DEV + chosen
    short_row = (chosen[0] + 1) % U_DEV
    drawn = drawn.at[short_row].set(low_bound)
    return drawn.at[full_rows].set(HIST)


def draw_user_query(key, part):
    base_vals = jax.random.normal(jax.random.fold_in(key, 21), (USERS, D), jnp.float32)
    return jnp.clip(base_vals, -1000.0, 1000.0).astype(jnp.bfloat16)


def place_ends(values, stream_key, smallest, largest):
    index_at = [jax.random.randint(jax.random.fold_in(stream_key, axis), (), 0, length) for axis, length in enumerate(values.shape)]
    longest = values.shape.index(max(values.shape))
    beside = index_at[:longest] + [(index_at[longest] + 1) % values.shape[longest]] + index_at[longest + 1:]
    return values.at[tuple(index_at)].set(smallest).at[tuple(beside)].set(largest)


def shard_levels(rng, shape, shards, least, top_value):
    def one(dim, parts):
        heights = jax.random.uniform(jax.random.fold_in(jax.random.fold_in(rng, 6), dim), (parts,), jnp.float32, least / len(shards), top_value / len(shards))
        return jnp.repeat(jnp.exp(heights), shape[dim] // parts).reshape((-1,) + (1,) * (len(shape) - dim - 1))

    gain = one(*shards[0])
    for cut in shards[1:]:
        gain = gain * one(*cut)
    return gain


def shared_out(key, own, number, rows, count, top, reach, skew):
    order = jax.random.permutation(key, count)
    packed, ordinary = load_shares(count, rows * top, reach, skew, True), load_shares(count, rows * top, reach, skew, False)
    places = jnp.arange(count)

    def named(sizes, offset_by):
        used = int((sizes > 0).sum())
        fixed = max(1, used // 4)
        passed = fixed + (places - fixed + offset_by * (used - fixed)) % max(1, count - fixed)
        return jnp.zeros((count,), jnp.int32).at[order[jnp.where(places < fixed, places, passed)]].set(jnp.asarray(sizes, jnp.int32))

    sizes = jnp.where(number % 4 == 0, named(packed, number // 4), named(ordinary, number - number // 4 - 1))
    mixed = jax.random.permutation(jax.random.fold_in(own, 3), count)
    giver, sink = mixed[0:count // 2 * 2:2], mixed[1:count // 2 * 2:2]
    margin = jnp.minimum(sizes[giver] - 1, reach - sizes[sink]) // 2
    margin = jnp.where((giver == order[0]) | (sink == order[0]) | (sizes[sink] == 0), 0, jnp.maximum(margin, 0))
    passed = jax.random.randint(jax.random.fold_in(own, 4), (count // 2,), 0, 1 << 20) % (margin + 1)
    sizes = sizes.at[giver].add(-passed).at[sink].add(passed)
    labels = jnp.searchsorted(jnp.cumsum(sizes), jnp.arange(rows * top), side="right").astype(jnp.int32)
    listing = labels.reshape(top, rows).T
    listing = listing[jax.random.permutation(jax.random.fold_in(own, 1), rows)]
    offset_by = jax.random.randint(jax.random.fold_in(own, 2), (rows, 1), 0, top)
    return jnp.take_along_axis(listing, (jnp.arange(top)[None, :] + offset_by) % top, axis=1)


def load_shares(amount, total, reach, skew, full):
    portions = [(1 << 20) // math.isqrt(rank ** skew) + 1 for rank in range(1, amount + 1)]
    largest = reach if full else min(reach, max(-(-total // amount), total * portions[0] // sum(portions)))
    least = 1 if total - largest >= amount - 1 else 0
    holding, spare = [largest] + [least] * (amount - 1), total - largest - least * (amount - 1)
    while spare > 0:
        free = [i for i in range(1, amount) if holding[i] < largest] or [i for i in range(1, amount) if holding[i] < reach]
        whole, budget = sum([portions[i] for i in free]), spare
        for i in free:
            more = min(reach - holding[i], max(1, budget * portions[i] // whole), spare)
            holding[i] = holding[i] + more
            spare = spare - more
    return np.array(holding)


def centred(key, extent, spread, limit, cuts=(), kind=jnp.bfloat16):
    values = spread * jax.random.normal(key, extent, jnp.float32)
    if cuts:
        values = values * shard_levels(key, extent, cuts, -0.22, 0.18)
    return jnp.clip(values, -limit, limit).astype(kind)


def setup_inputs(seed: int = 0) -> dict:
    seeds = jax.random.split(jax.random.key(seed), 12)
    history = centred(seeds[0], (USERS, HIST, D), 1.0, 6.0, ((0, 256),))
    lengths = draw_lengths(jax.random.fold_in(seeds[11], 71), 0)
    user_query = draw_user_query(jax.random.fold_in(seeds[11], 71), 0)
    pos_item = centred(seeds[3], (USERS, D), 1.0, 6.0, ((0, 256),))
    neg_index = place_ends(jax.random.randint(seeds[4], (USERS, NEG), 0, USERS), jax.random.fold_in(seeds[4], 1), 0, USERS - 1).astype(jnp.int32)
    routes_keys = jax.random.split(jax.random.fold_in(seeds[5], 1), ROWS // (U_DEV * CANDS))
    routes_turns = jax.random.permutation(jax.random.fold_in(seeds[5], 3), ROWS // (U_DEV * CANDS))
    routes = jax.vmap(lambda own, number: shared_out(jax.random.fold_in(seeds[5], 2), own, number, U_DEV * CANDS, EXPERTS, 2, CAP, 2))(routes_keys, routes_turns).reshape((ROWS, 2))
    w_router = centred(seeds[6], (D, EXPERTS), D ** -0.5, 0.125)
    w_gate = centred(seeds[7], (EXPERTS, D, FF), D ** -0.5, 0.125, ((0, 16), (1, 16)))
    w_up = centred(seeds[8], (EXPERTS, D, FF), D ** -0.5, 0.125, ((0, 16), (1, 16)))
    w_down = centred(seeds[9], (EXPERTS, FF, D), FF ** -0.5, 0.21875, ((0, 16), (2, 16)))
    out_gain = jnp.clip(1.0 + 0.15 * jax.random.normal(seeds[10], (D,), jnp.float32), 0.25, 1.75)
    return {"history": history, "lengths": lengths, "user_query": user_query, "pos_item": pos_item, "neg_index": neg_index, "routes": routes, "w_router": w_router, "w_gate": w_gate, "w_up": w_up, "w_down": w_down, "out_gain": out_gain}


norm_eps = 1e-06
loss_scale = 1024.0

def silu_pair(pre_act):
    sigma_val = jax.nn.sigmoid(pre_act)
    return (pre_act * sigma_val, sigma_val * (1.0 + pre_act * (1.0 - sigma_val)))

def rms_round(values):
    scale_inv = lax.rsqrt(lax.optimization_barrier(jnp.mean(values * values, axis=-1, keepdims=True)) + norm_eps)
    return (values * scale_inv).astype(jnp.bfloat16)

def pool_user(block_args):
    hist_rows, hist_len, query_row = block_args
    keys_f = hist_rows.astype(jnp.float32).reshape(HIST, HEADS, HEAD)
    query_f = query_row.astype(jnp.float32).reshape(HEADS, HEAD)
    scores = jnp.einsum('hd,thd->ht', query_f, keys_f) / math.sqrt(HEAD)
    live_mask = (jnp.arange(HIST, dtype=jnp.int32) < hist_len)[None, :]
    scores = jnp.where(live_mask, scores, -1e+30)
    top_val = lax.optimization_barrier(jnp.max(scores, axis=-1, keepdims=True))
    weights = jnp.where(live_mask, jnp.exp(scores - top_val), 0.0)
    attn_probs = (weights / lax.optimization_barrier(jnp.sum(weights, axis=-1, keepdims=True))).astype(jnp.bfloat16)
    pooled = jnp.einsum('ht,thd->hd', attn_probs.astype(jnp.float32), keys_f)
    return pooled.reshape(D)

def reference(history, lengths, user_query, pos_item, neg_index, routes, w_router, w_gate, w_up, w_down, out_gain):
    context = lax.map(pool_user, (history, lengths, user_query))
    candidates = jnp.concatenate([pos_item[:, None, :], pos_item[neg_index]], axis=1)
    x_sum = candidates.astype(jnp.float32) + context[:, None, :]
    normed = rms_round(x_sum).reshape(ROWS, D)
    logits = jnp.dot(normed, w_router, preferred_element_type=jnp.float32)
    affinity = jax.nn.sigmoid(jnp.take_along_axis(logits, routes, axis=1))
    aff_total = lax.optimization_barrier(jnp.sum(affinity, axis=1, keepdims=True))
    mix = affinity / aff_total
    per_dev = 2 * CANDS * U_DEV
    n_devices = N_DP * N_EXPERT
    slot_count = N_EXPERT * CAP
    flat_routes = routes.reshape(n_devices, per_dev)
    one_hot = (flat_routes[..., None] == jnp.arange(EXPERTS, dtype=jnp.int32)).astype(jnp.int32)
    slot_rank = lax.optimization_barrier(jnp.sum(jnp.cumsum(one_hot, axis=1) * one_hot, axis=-1)) - 1
    device_ids = jnp.arange(n_devices, dtype=jnp.int32)[:, None] + jnp.zeros_like(flat_routes)
    group_ids = device_ids // N_EXPERT
    buffer_pos = device_ids % N_EXPERT * CAP + slot_rank
    assign_ids = jnp.arange(n_devices * per_dev, dtype=jnp.int32).reshape(n_devices, per_dev)
    table = jnp.full((EXPERTS, N_DP, slot_count), -1, jnp.int32)
    table = table.at[flat_routes, group_ids, buffer_pos].set(assign_ids)

    def expert_block(expert_id, slot_ids):
        live_mask = (slot_ids >= 0)[:, None]
        rows_in = jnp.where(live_mask, normed[jnp.maximum(slot_ids, 0) // 2], jnp.zeros((), jnp.bfloat16))
        gate_pre = jnp.dot(rows_in, w_gate[expert_id], preferred_element_type=jnp.float32)
        up_pre = jnp.dot(rows_in, w_up[expert_id], preferred_element_type=jnp.float32)
        silu_val, silu_grad = silu_pair(gate_pre)
        hidden = (silu_val * up_pre).astype(jnp.bfloat16)
        return (live_mask, rows_in, up_pre, silu_val, silu_grad, hidden)

    def forward_block(block_args):
        expert_id, slot_ids = block_args
        hidden = expert_block(expert_id, slot_ids)[5]
        return jnp.dot(hidden, w_down[expert_id], preferred_element_type=jnp.float32).astype(jnp.bfloat16)
    expert_of = jnp.arange(EXPERTS * N_DP, dtype=jnp.int32) // N_DP
    block_outs = lax.map(forward_block, (expert_of, table.reshape(EXPERTS * N_DP, slot_count)))
    expert_out = block_outs[flat_routes * N_DP + group_ids, buffer_pos].reshape(ROWS, 2, D)
    moe_sum = mix[:, 0:1] * expert_out[:, 0].astype(jnp.float32) + mix[:, 1:2] * expert_out[:, 1].astype(jnp.float32)
    h_rows = (x_sum.reshape(ROWS, D) + moe_sum).reshape(USERS, CANDS, D)
    inv_rms = lax.rsqrt(lax.optimization_barrier(jnp.mean(h_rows * h_rows, axis=-1, keepdims=True)) + norm_eps)
    unit_rows = h_rows * inv_rms
    scored = unit_rows * out_gain
    query_f = user_query.astype(jnp.float32)
    listwise = jnp.einsum('ucd,ud->uc', scored, query_f, precision=lax.Precision.HIGHEST) / math.sqrt(D)
    top_val = lax.optimization_barrier(jnp.max(listwise, axis=-1, keepdims=True))
    expo = jnp.exp(listwise - top_val)
    expo_total = lax.optimization_barrier(jnp.sum(expo, axis=-1, keepdims=True))
    losses = jnp.log(expo_total[:, 0]) + top_val[:, 0] - listwise[:, 0]
    first_one = (jnp.arange(CANDS, dtype=jnp.int32) == 0).astype(jnp.float32)[None, :]
    d_list = loss_scale * (expo / expo_total - first_one)
    d_scored = d_list[..., None] * query_f[:, None, :] / math.sqrt(D)
    d_unit = d_scored * out_gain
    d_h = inv_rms * (d_unit - unit_rows * lax.optimization_barrier(jnp.mean(d_unit * unit_rows, axis=-1, keepdims=True)))
    d_h = d_h.reshape(ROWS, D)
    d_out = (mix[:, :, None] * d_h[:, None, :]).astype(jnp.bfloat16)
    d_mix = lax.optimization_barrier(jnp.sum(d_h[:, None, :] * expert_out.astype(jnp.float32), axis=-1))
    mix_dot = lax.optimization_barrier(jnp.sum(mix * d_mix, axis=1, keepdims=True))
    d_aff = (d_mix - mix_dot) / aff_total
    d_pick = d_aff * affinity * (1.0 - affinity)
    route_hot = (routes[:, :, None] == jnp.arange(EXPERTS, dtype=jnp.int32)).astype(jnp.float32)
    d_logits = lax.optimization_barrier(jnp.sum(route_hot * d_pick[:, :, None], axis=1)).astype(jnp.bfloat16)
    grad_router = jnp.dot(normed.T, d_logits, preferred_element_type=jnp.float32)
    d_flat = d_out.reshape(ROWS * 2, D)

    def expert_grads(expert_id):

        def per_group(running, slot_ids):
            live_mask, rows_in, up_pre, silu_val, silu_grad, hidden = expert_block(expert_id, slot_ids)
            grad_rows = jnp.where(live_mask, d_flat[jnp.maximum(slot_ids, 0)], jnp.zeros((), jnp.bfloat16))
            d_hidden = jnp.dot(grad_rows, w_down[expert_id].T, preferred_element_type=jnp.float32)
            d_gate = (d_hidden * up_pre * silu_grad).astype(jnp.bfloat16)
            d_up = (d_hidden * silu_val).astype(jnp.bfloat16)
            part_gate = jnp.dot(rows_in.T, d_gate, preferred_element_type=jnp.float32).astype(jnp.bfloat16)
            part_up = jnp.dot(rows_in.T, d_up, preferred_element_type=jnp.float32).astype(jnp.bfloat16)
            part_down = jnp.dot(hidden.T, grad_rows, preferred_element_type=jnp.float32).astype(jnp.bfloat16)
            part_gate, part_up, part_down = lax.optimization_barrier((part_gate, part_up, part_down))
            return ((running[0] + part_gate.astype(jnp.float32), running[1] + part_up.astype(jnp.float32), running[2] + part_down.astype(jnp.float32)), None)
        init = (jnp.zeros((D, FF), jnp.float32), jnp.zeros((D, FF), jnp.float32), jnp.zeros((FF, D), jnp.float32))
        summed, _ = lax.scan(per_group, init, table[expert_id])
        return summed
    grad_gate, grad_up, grad_down = lax.map(expert_grads, jnp.arange(EXPERTS, dtype=jnp.int32))
    return (losses, grad_gate, grad_up, grad_down, grad_router)
```

```python
import functools
import math

import jax
import jax.numpy as jnp
from jax import lax
from jax.experimental import pallas as pl
from jax.experimental.pallas import tpu as pltpu
from jax.sharding import PartitionSpec as P

HEAD = 128
CANDS = 64
EPS = 1e-6
LOSS_SCALE = 1024.0
LANES = 128

f32, bf16, i32 = jnp.float32, jnp.bfloat16, jnp.int32
NT = (((1,), (1,)), ((), ()))
TN = (((0,), (0,)), ((), ()))


def dot(a, b):
    return jnp.dot(a, b, preferred_element_type=f32)


def iota(shape, dim):
    return lax.broadcasted_iota(i32, shape, dim)


def kernel(
    sizes,
    hist, lens, q_ref, pos_ref, lane_ints, col_ints, wr_ref, wg, wu, wd, gain_ref,
    loss_out, gg_out, gu_out, gd_out, gr_out,
    bufs, w_g, w_u, w_d, tab, pieces, ctx_pieces, ctx2, codes_out, codes,
    s01, st, xh, nloc, gq_ref, xbuf, rows, rows_t, acc_g, acc_u, acc_h,
    hid, hid_t, d_gu, r_part, r_got, r_mid, r_fin,
    g_own, g_out, g_sib, d_own, d_out, d_sib, g_ring, d_ring,
    hist_sem, own_sem, small_s, small_r, ring_s, ring_r, sib_s, sib_r,
    a_s, a_r, gsib_s, gsib_r, dsib_s, dsib_r, sum_s, sum_r,
):
    Z, E, D, FF, CAP, R = (sizes[k] for k in ("Z", "E", "D", "FF", "CAP", "R"))
    S = E * CAP
    HEADS = D // HEAD
    PC = LANES
    NP = D // PC
    PR = 2 * NP
    FH = FF // 2
    N_ITEMS = 2 * E * 2 * Z
    HALF = N_ITEMS // 2
    BLK = 2 * Z
    TABW = tab.shape[0]
    CH = 2 * LANES

    dp = lax.axis_index("dp")
    me = lax.axis_index("expert")
    z = lax.div(dp, 2)
    c = lax.rem(dp, 2)
    sib_dp = 2 * z + 1 - c

    def at_z(off):
        return lax.rem(z + (off + Z), Z)

    def peer(j):
        if E == 16:
            x, y = lax.div(me, 4), lax.rem(me, 4)
            return lax.rem(x + lax.div(j, 4), 4) * 4 + lax.rem(y + lax.rem(j, 4), 4)
        return lax.rem(me + j, E)

    def mo(v, n):
        return pl.multiple_of(v, n)

    def remote(src, dst, s_sem, r_sem, to_dp, to_e):
        return pltpu.make_async_remote_copy(
            src_ref=src, dst_ref=dst, send_sem=s_sem, recv_sem=r_sem,
            device_id={"dp": to_dp, "expert": to_e},
            device_id_type=pl.DeviceIdType.MESH,
        )

    def took(ref, sem):
        pltpu.make_async_copy(ref, ref, sem).wait()

    def to_peers(make):
        @pl.loop(1, E)
        def _(j):
            make(peer(j)).start()

    drains = []

    hist_copies = [
        pltpu.make_async_copy(hist.at[n // 2, pl.ds((n % 2) * S, S), :], bufs.at[n], hist_sem.at[n])
        for n in range(4)
    ]
    for cp in hist_copies:
        cp.start()

    own = (wg.at[0], wu.at[0], wd.at[0, pl.ds(0, FH), :], wd.at[0, pl.ds(FH, FH), :])

    def wref(t, of):
        if t < 2:
            return (w_g, w_u)[t].at[pl.ds(mo(of * LANES, LANES), LANES), :]
        return w_d.at[pl.ds((t - 2) * FH, FH), pl.ds(mo(of * LANES, LANES), LANES)]

    own_copies = [pltpu.make_async_copy(own[t], wref(t, dp), own_sem.at[t]) for t in range(4)]
    for cp in own_copies:
        cp.start()

    pos = pos_ref[...].astype(f32)
    for u in range(2):
        for j in range(NP):
            pieces[pl.ds(z * PR + NP * u + j, 1), :] = pos[u : u + 1, j * PC : (j + 1) * PC]

    barrier = pltpu.get_barrier_semaphore()

    @pl.loop(1, E)
    def _(j):
        pl.semaphore_signal(
            barrier, inc=1, device_id={"dp": dp, "expert": peer(j)},
            device_id_type=pl.DeviceIdType.MESH,
        )

    @pl.loop(1, 2 * Z)
    def _(j):
        pl.semaphore_signal(
            barrier, inc=1, device_id={"dp": lax.rem(dp + j, 2 * Z), "expert": me},
            device_id_type=pl.DeviceIdType.MESH,
        )

    pl.semaphore_wait(barrier, E - 1 + 2 * Z - 1)

    HOPS = [(Z // 2, Z // 2 - 1), (Z // 2 - 1, Z // 2)] * 2

    def ring_send(t, d, k, src, dst):
        cp = remote(
            src, dst, ring_s.at[t, d, k], ring_r.at[t, d, k],
            2 * at_z(1 if d == 0 else -1) + c, me,
        )
        cp.start()
        drains.append(cp.wait_send)

    def sib_send(t, idx, src, dst):
        cp = remote(src, dst, sib_s.at[t, idx], sib_r.at[t, idx], sib_dp, me)
        cp.start()
        drains.append(cp.wait_send)

    def ring_begin(types):
        for t in types:
            for d in range(2):
                if HOPS[t][d] > 0:
                    ring_send(t, d, 0, own[t], wref(t, dp))
        for t in types:
            sib_send(t, 0, own[t], wref(t, dp))

    def ring_event(types, k):
        for t in types:
            for d in range(2):
                if k > HOPS[t][d]:
                    continue
                off = -k if d == 0 else k
                r = wref(t, 2 * at_z(off) + c)
                took(r, ring_r.at[t, d, k - 1])
                if k < HOPS[t][d]:
                    ring_send(t, d, k, r, r)
                sib_send(t, off % Z, r, r)

    def sib_wait(types, off):
        for t in types:
            took(wref(t, 2 * at_z(off) + 1 - c), sib_r.at[t, off % Z])

    my_piece = pieces.at[pl.ds(mo(z * PR, PR), PR), :]

    @pl.loop(1, Z)
    def _(k):
        remote(
            my_piece, my_piece, small_s.at[0], small_r.at[0],
            2 * lax.rem(z + k, Z) + c, me,
        ).start()

    drains.append(lambda: took(pieces.at[pl.ds(0, (Z - 1) * PR), :], small_s.at[0]))
    ring_begin((0, 1))

    rt0, rt1 = lane_ints[0:1, :], lane_ints[1:2, :]
    id_lane = lane_ints[2:3, :]

    def table_row(i):
        dev = lax.shift_right_logical(i, 1)
        of = lax.div(dev, E)
        return (
            lax.rem(of, 2) * HALF + lax.rem(dev, E) * BLK + lax.div(of, 2) * 2 + (i & 1)
        )

    e_sub = iota((E, R), 0)
    mt0, mt1 = e_sub == rt0, e_sub == rt1
    upper = (iota((R, R), 0) < iota((R, R), 1)).astype(bf16)
    rank_t = dot((mt0 | mt1).astype(bf16), upper) + (CAP * e_sub).astype(f32)
    slot0 = jnp.sum(jnp.where(mt0, rank_t, 0.0), axis=0, keepdims=True).astype(i32)
    slot1 = jnp.sum(jnp.where(mt1, rank_t, 0.0), axis=0, keepdims=True).astype(i32)
    s_sub = iota((S, R), 0)
    in0, in1 = s_sub == slot0, s_sub == slot1
    s01[:, 0:R] = in0.astype(bf16)
    s01[:, R : 2 * R] = in1.astype(bf16)
    user_lane = me * 2 + (iota((1, R), 1) >= CANDS).astype(i32)
    code_lane = (table_row(id_lane) + user_lane * N_ITEMS + 1).astype(f32)
    code = jnp.sum(jnp.where(in0 | in1, code_lane, 0.0), axis=1, keepdims=True).astype(i32) - 1
    codes_out[...] = jnp.broadcast_to(code, (S, LANES))
    my_slots = pl.ds(mo(me * CAP, CAP), CAP)
    codes[my_slots, :] = codes_out[my_slots, :]
    to_peers(
        lambda p: remote(
            codes_out.at[pl.ds(mo(p * CAP, CAP), CAP), :], codes.at[my_slots, :],
            small_s.at[1], small_r.at[1], dp, p,
        )
    )
    drains.append(lambda: took(codes_out.at[pl.ds(0, S - CAP), :], small_s.at[1]))

    r0, r1, id_col = col_ints[:, 0:1], col_ints[:, 1:2], col_ints[:, 2:3]
    e_lane = iota((R, E), 1)
    m0, m1 = e_lane == r0, e_lane == r1
    lower = (iota((R, R), 1) < iota((R, R), 0)).astype(bf16)
    rank = dot(lower, (m0 | m1).astype(bf16)) + (CAP * e_lane).astype(f32)
    s_lane = iota((R, S), 1)
    for k, m in enumerate((m0, m1)):
        slot = jnp.sum(jnp.where(m, rank, 0.0), axis=1, keepdims=True).astype(i32)
        st[k * R : (k + 1) * R, :] = (s_lane == slot).astype(bf16)

    took(pieces.at[pl.ds(0, (Z - 1) * PR), :], small_r.at[0])
    my_block = pl.ds(mo(c * HALF + me * BLK, BLK), BLK)
    for j in range(NP):
        tab[my_block, j * PC : (j + 1) * PC] = pieces[pl.ds(j, BLK, stride=NP), :].astype(bf16)
    to_peers(
        lambda p: remote(
            tab.at[my_block, :], tab.at[my_block, :], small_s.at[2], small_r.at[2], dp, p
        )
    )
    drains.append(lambda: took(tab.at[pl.ds(0, (E - 1) * BLK), :], small_s.at[2]))

    in_head = lax.shift_right_logical(iota((HEADS, D), 1), 7) == iota((HEADS, D), 0)

    def attend(u):
        hist_copies[2 * u].wait()
        hist_copies[2 * u + 1].wait()
        qd = jnp.where(in_head, q_ref[u : u + 1, :].astype(f32), 0.0).astype(bf16)
        halves, tops = [], []
        for n in range(2):
            s = lax.dot_general(qd, bufs[2 * u + n], NT, preferred_element_type=f32)
            s = s * (1.0 / math.sqrt(HEAD))
            live = (iota((HEADS, S), 1) + n * S) < lens[u]
            s = jnp.where(live, s, -1e30)
            halves.append((s, live))
            tops.append(jnp.max(s, axis=1, keepdims=True))
        top = jnp.maximum(tops[0], tops[1])
        w = [jnp.where(live, jnp.exp(s - top), 0.0) for s, live in halves]
        total = jnp.sum(w[0], axis=1, keepdims=True) + jnp.sum(w[1], axis=1, keepdims=True)
        pooled = dot((w[0] / total).astype(bf16), bufs[2 * u]) + dot(
            (w[1] / total).astype(bf16), bufs[2 * u + 1]
        )
        ctx = jnp.sum(jnp.where(in_head, pooled, 0.0), axis=0, keepdims=True)
        ctx2[u : u + 1, :] = ctx
        for j in range(NP):
            ctx_pieces[pl.ds(me * PR + NP * u + j, 1), :] = ctx[:, j * PC : (j + 1) * PC]

    attend(0)
    ring_event((0, 1), 1)
    attend(1)
    my_ctx = ctx_pieces.at[pl.ds(mo(me * PR, PR), PR), :]
    to_peers(lambda p: remote(my_ctx, my_ctx, small_s.at[3], small_r.at[3], dp, p))
    drains.append(lambda: took(ctx_pieces.at[pl.ds(0, (E - 1) * PR), :], small_s.at[3]))

    took(tab.at[pl.ds(0, (E - 1) * BLK), :], small_r.at[2])
    my_half = tab.at[pl.ds(mo(c * HALF, HALF), HALF), :]
    half_copy = remote(my_half, my_half, small_s.at[4], small_r.at[4], sib_dp, me)
    half_copy.start()
    drains.append(half_copy.wait_send)
    for u in range(2):
        gq_ref[u : u + 1, :] = q_ref[u : u + 1, :].astype(f32) * gain_ref[...]
    ring_event((0, 1), 2)
    took(my_half, small_r.at[4])

    first_user = iota((R, 1), 0) < CANDS

    def by_user(ref, cols):
        return jnp.where(first_user, ref[0:1, cols], ref[1:2, cols])

    oh = (iota((R, N_ITEMS), 1) == table_row(id_col)).astype(bf16)
    NC = min(512, D)
    total = jnp.zeros((R, 1), f32)
    for n in range(D // NC):
        cols = slice(n * NC, (n + 1) * NC)
        x = dot(oh, tab[0:N_ITEMS, cols]) + by_user(ctx2, cols)
        xh[:, cols] = x
        total = total + jnp.sum(x * x, axis=1, keepdims=True)
    inv = lax.rsqrt(total * (1.0 / D) + EPS)
    for n in range(D // NC):
        cols = slice(n * NC, (n + 1) * NC)
        nloc[:, cols] = (xh[:, cols] * inv).astype(bf16)
    logits = lax.dot_general(nloc[...], wr_ref[...], NT, preferred_element_type=f32)
    affinity = jax.nn.sigmoid(logits)
    aff0 = jnp.sum(jnp.where(m0, affinity, 0.0), axis=1, keepdims=True)
    aff1 = jnp.sum(jnp.where(m1, affinity, 0.0), axis=1, keepdims=True)
    aff_total = aff0 + aff1
    mix0, mix1 = aff0 / aff_total, aff1 / aff_total

    took(ctx_pieces.at[pl.ds(0, (E - 1) * PR), :], small_r.at[3])
    NU = 2 * E
    for j in range(NP):
        cols = slice(j * PC, (j + 1) * PC)
        v = ctx_pieces[pl.ds(j, NU, stride=NP), :]
        for n in range(3):
            part = v.astype(bf16)
            tab[N_ITEMS + n * NU : N_ITEMS + (n + 1) * NU, cols] = part
            v = v - part.astype(f32)
    tab[N_ITEMS + 3 * NU :, :] = jnp.zeros((TABW - N_ITEMS - 3 * NU, D), bf16)
    took(codes.at[pl.ds(0, S - CAP), :], small_r.at[1])
    ring_event((0, 1), 3) if Z > 6 else None
    MT = min(128, S)

    @pl.loop(0, S // MT)
    def _(m):
        here = pl.ds(mo(m * MT, MT), MT)
        got = codes[here, :]
        item = jnp.where(got >= 0, got & (N_ITEMS - 1), -1)
        user = lax.shift_right_arithmetic(got, N_ITEMS.bit_length() - 1)
        lane = iota((MT, LANES), 1)
        parts = [(item == lane + LANES * b).astype(bf16) for b in range(max(1, N_ITEMS // LANES))]
        if N_ITEMS < LANES:
            parts = [p[:, :N_ITEMS] for p in parts]
        parts.append(((user == lax.rem(lane, NU)) & (lane < 3 * NU)).astype(bf16))
        hot = jnp.concatenate(parts, axis=1)
        ss = jnp.zeros((MT, 1), f32)
        for n in range(D // NC):
            cols = slice(n * NC, (n + 1) * NC)
            x = dot(hot, tab[:, cols])
            xbuf[:, cols] = x
            ss = ss + jnp.sum(x * x, axis=1, keepdims=True)
        scale = lax.rsqrt(ss * (1.0 / D) + EPS)
        for n in range(D // NC):
            cols = slice(n * NC, (n + 1) * NC)
            y = (xbuf[:, cols] * scale).astype(bf16)
            rows[here, cols] = y
            rows_t[cols, here] = y.T

    for k in range(3, Z // 2 + 1) if Z <= 6 else range(4, Z // 2 + 1):
        ring_event((0, 1), k)
    ring_begin((2, 3))

    near_first = [0]
    for k in range(1, Z // 2):
        near_first += [k, -k]
    near_first.append(Z // 2)
    FT = 256

    for off in near_first:
        if off == 0:
            own_copies[0].wait()
            own_copies[1].wait()
        sib_wait((0, 1), off)
        cols = pl.ds(mo(at_z(off) * CH, CH), CH)

        @pl.loop(0, FF // FT)
        def _(n):
            f = pl.ds(mo(n * FT, FT), FT)
            left = rows[:, cols]
            for acc, w in ((acc_g, w_g), (acc_u, w_u)):
                v = dot(left, w[cols, f])
                if off == 0:
                    acc[:, f] = v
                else:
                    acc[:, f] += v

    @pl.loop(0, S // 64)
    def _(m):
        here = pl.ds(mo(m * 64, 64), 64)
        g, up = acc_g[here, :], acc_u[here, :]
        sig = jax.nn.sigmoid(g)
        silu = g * sig
        hid[here, :] = (silu * up).astype(bf16)
        acc_g[here, :] = up * (sig * (1.0 + g * (1.0 - sig)))
        acc_u[here, :] = silu

    def exchange(way, i, cols, src, dst):
        to_peers(
            lambda p: remote(
                bufs.at[src, pl.ds(mo(p * CAP, CAP), CAP), cols], bufs.at[dst, my_slots, cols],
                a_s.at[way, i], a_r.at[way, i], dp, p,
            )
        )
        drains.append(lambda: took(bufs.at[src, pl.ds(0, S - CAP), cols], a_s.at[way, i]))

    done_k = 0
    for i, off in enumerate(near_first):
        if off == 0:
            own_copies[2].wait()
            own_copies[3].wait()
        if abs(off) > done_k:
            done_k = abs(off)
            ring_event((2, 3), done_k)
        sib_wait((2, 3), off)
        cols = pl.ds(mo(at_z(off) * CH, CH), CH)
        bufs[0, :, cols] = dot(hid[...], w_d[:, cols]).astype(bf16)
        bufs[1, my_slots, cols] = bufs[0, my_slots, cols]
        exchange(0, i, cols, 0, 1)

    for n in range(FF // LANES):
        f = slice(n * LANES, (n + 1) * LANES)
        hid_t[f, :] = hid[:, f].T

    sums = [jnp.zeros((R, 1), f32) for _ in range(6)]
    for i, off in enumerate(near_first):
        cols = pl.ds(mo(at_z(off) * CH, CH), CH)
        took(bufs.at[1, pl.ds(0, S - CAP), cols], a_r.at[0, i])
        e = dot(st[...], bufs[1, :, cols])
        e0, e1 = e[0:R], e[R : 2 * R]
        h = xh[:, cols] + mix0 * e0 + mix1 * e1
        xh[:, cols] = h
        gq = by_user(gq_ref, cols)
        terms = (h * h, h * gq, gq * e0, gq * e1, h * e0, h * e1)
        sums = [a + jnp.sum(t, axis=1, keepdims=True) for a, t in zip(sums, terms)]
    hh, hq, qe0, qe1, he0, he1 = sums

    inv_h = lax.rsqrt(hh * (1.0 / D) + EPS)
    listwise = hq * inv_h * (1.0 / math.sqrt(D))
    d_parts = []
    for u in range(2):
        lw = listwise[u * CANDS : (u + 1) * CANDS]
        top = jnp.max(lw, axis=0, keepdims=True)
        ex = jnp.exp(lw - top)
        ex_total = jnp.sum(ex, axis=0, keepdims=True)
        loss = jnp.log(ex_total) + top - lw[0:1]
        loss_out[u : u + 1, :] = jnp.broadcast_to(loss, (1, LANES))
        first = (iota((CANDS, 1), 0) == 0).astype(f32)
        d_parts.append(LOSS_SCALE * (ex / ex_total - first))
    d_list = jnp.concatenate(d_parts, axis=0) * (1.0 / math.sqrt(D))
    alpha = inv_h * d_list
    beta = alpha * inv_h * inv_h * hq * (1.0 / D)

    far_first = near_first[::-1]
    for i, off in enumerate(far_first):
        cols = pl.ds(mo(at_z(off) * CH, CH), CH)
        dh = alpha * by_user(gq_ref, cols) - beta * xh[:, cols]
        both = jnp.concatenate([(mix0 * dh).astype(bf16), (mix1 * dh).astype(bf16)], axis=0)
        bufs[2, :, cols] = dot(s01[...], both).astype(bf16)
        bufs[3, my_slots, cols] = bufs[2, my_slots, cols]
        exchange(1, i, cols, 2, 3)

    d_mix0, d_mix1 = alpha * qe0 - beta * he0, alpha * qe1 - beta * he1
    mix_dot = mix0 * d_mix0 + mix1 * d_mix1
    pick0 = (d_mix0 - mix_dot) / aff_total * aff0 * (1.0 - aff0)
    pick1 = (d_mix1 - mix_dot) / aff_total * aff1 * (1.0 - aff1)
    d_logits = (jnp.where(m0, pick0, 0.0) + jnp.where(m1, pick1, 0.0)).astype(bf16)
    DB = D // E
    r_part[...] = lax.dot_general(d_logits, nloc[...], TN, preferred_element_type=f32)
    my_cols = pl.ds(mo(me * DB, DB), DB)
    r_got[me] = r_part[:, my_cols]
    to_peers(
        lambda p: remote(
            r_part.at[:, pl.ds(mo(p * DB, DB), DB)], r_got.at[me],
            small_s.at[5], small_r.at[5], dp, p,
        )
    )
    drains.append(lambda: took(r_got.at[pl.ds(0, E - 1)], small_s.at[5]))

    def ring_slot(t, d, k):
        return g_ring.at[t, d, k] if t < 2 else d_ring.at[t - 2, d, k]

    def block(three, t, of):
        if t < 2:
            return three[0].at[t, pl.ds(mo(of * LANES, LANES), LANES), :]
        return three[1].at[of, pl.ds((t - 2) * FH, FH), :]

    mine = (g_own, d_own)
    theirs = (g_sib, d_sib)

    def add_rows(t, of, extra, out):
        height = LANES if t < 2 else FH
        step = 64

        @pl.loop(0, height // step)
        def _(m):
            here = pl.ds(mo(m * step, step), step)
            a, b = block(mine, t, of), block(theirs, t, of)
            v = a[here, :].astype(f32) + b[here, :].astype(f32)
            for r in extra:
                v = v + r[here, :].astype(f32)
            if out is None:
                a[here, :] = v.astype(bf16)
            else:
                out[here, :] = v

    def sum_send(t, d, k):
        of = at_z(k if d == 0 else -k)
        extra = []
        if k < HOPS[t][d]:
            r = ring_slot(t, d, k)
            took(r, sum_r.at[t, d, k])
            extra.append(r)
        add_rows(t, of, extra, None)
        cp = remote(
            block(mine, t, of), ring_slot(t, d, k - 1), sum_s.at[t, d, k - 1],
            sum_r.at[t, d, k - 1], 2 * at_z(1 if d == 0 else -1) + c, me,
        )
        cp.start()
        drains.append(cp.wait_send)

    def sum_step(types, k):
        for t in types:
            for d in range(2):
                if k <= HOPS[t][d]:
                    sum_send(t, d, k)

    def sum_last(t, out):
        extra = []
        for d in range(2):
            if HOPS[t][d] > 0:
                r = ring_slot(t, d, 0)
                took(r, sum_r.at[t, d, 0])
                extra.append(r)
        add_rows(t, z, extra, out)

    def down_wait(off):
        took(d_sib.at[at_z(off)], dsib_r.at[off % Z])

    def gate_wait(off):
        for t in range(2):
            took(block(theirs, t, at_z(off)), gsib_r.at[t, off % Z])

    def offs_at(k):
        if k == 0 or k == Z // 2:
            return [k]
        return [k, -k]

    i = 0
    for k in range(Z // 2, -1, -1):
        for off in reversed(offs_at(k)):
            of = at_z(off)
            cols = pl.ds(mo(of * CH, CH), CH)
            took(bufs.at[3, pl.ds(0, S - CAP), cols], a_r.at[1, i])
            got = bufs[3, :, cols]
            v = lax.dot_general(got, w_d[:, cols], NT, preferred_element_type=f32)
            if i == 0:
                acc_h[...] = v
            else:
                acc_h[...] += v
            g = dot(hid_t[...], got)
            low, high = g[:, :LANES], g[:, LANES:]
            d_own[of] = jnp.where(c == 0, low, high).astype(bf16)
            d_out[of] = jnp.where(c == 0, high, low).astype(bf16)
            cp = remote(d_out.at[of], d_sib.at[of], dsib_s.at[off % Z], dsib_r.at[off % Z], sib_dp, me)
            cp.start()
            drains.append(cp.wait_send)
            i += 1
        if k + 1 <= Z // 2:
            for off in offs_at(k + 1):
                down_wait(off)
            sum_step((2, 3), k + 1)

    @pl.loop(0, S // 64)
    def _(m):
        here = pl.ds(mo(m * 64, 64), 64)
        dh = acc_h[here, :]
        d_gu[0, here, :] = (dh * acc_g[here, :]).astype(bf16)
        d_gu[1, here, :] = (dh * acc_u[here, :]).astype(bf16)

    took(r_got.at[pl.ds(0, E - 1)], small_r.at[5])
    part = r_got[0]
    for n in range(1, E):
        part = part + r_got[n]
    r_mid[dp] = part

    @pl.loop(1, 2 * Z)
    def _(j):
        remote(
            r_mid.at[dp], r_mid.at[dp], small_s.at[6], small_r.at[6],
            lax.rem(dp + j, 2 * Z), me,
        ).start()

    drains.append(lambda: took(r_mid.at[pl.ds(0, 2 * Z - 1)], small_s.at[6]))

    for k in range(Z // 2, -1, -1):
        for off in reversed(offs_at(k)):
            of = at_z(off)
            for core, dest in ((c, g_own), (1 - c, g_out)):
                at = pl.ds(mo((2 * of + core) * LANES, LANES), LANES)
                to = pl.ds(mo(of * LANES, LANES), LANES)
                left = rows_t[at, :]
                for t in range(2):
                    dest[t, to, :] = dot(left, d_gu[t]).astype(bf16)
            for t in range(2):
                cp = remote(
                    block((g_out, d_out), t, of), block(theirs, t, of),
                    gsib_s.at[t, off % Z], gsib_r.at[t, off % Z], sib_dp, me,
                )
                cp.start()
                drains.append(cp.wait_send)
        if k + 1 <= Z // 2:
            for off in offs_at(k + 1):
                gate_wait(off)
            sum_step((0, 1), k + 1)

    down_wait(0)
    sum_last(2, gd_out.at[pl.ds(0, FH), :])
    sum_last(3, gd_out.at[pl.ds(FH, FH), :])

    took(r_mid.at[pl.ds(0, 2 * Z - 1)], small_r.at[6])
    part = r_mid[0]
    for n in range(1, 2 * Z):
        part = part + r_mid[n]
    r_fin[me] = part
    to_peers(
        lambda p: remote(r_fin.at[me], r_fin.at[me], small_s.at[7], small_r.at[7], dp, p)
    )
    drains.append(lambda: took(r_fin.at[pl.ds(0, E - 1)], small_s.at[7]))
    took(r_fin.at[pl.ds(0, E - 1)], small_r.at[7])
    for n in range(E):
        gr_out[:, n * DB : (n + 1) * DB] = r_fin[n]

    gate_wait(0)
    sum_last(0, gg_out)
    sum_last(1, gu_out)
    for drain in drains:
        drain()


def local(
    sizes, history, lengths, user_query, pos_item, neg_index, routes,
    w_router, w_gate, w_up, w_down, out_gain,
):
    Z, E, D, FF, CAP, R = (sizes[k] for k in ("Z", "E", "D", "FF", "CAP", "R"))
    S = E * CAP
    base = (lax.axis_index("dp") * E + lax.axis_index("expert")) * 2
    ids = jnp.concatenate(
        [base + jnp.arange(2, dtype=i32)[:, None], neg_index], axis=1
    ).reshape(R)
    lane_ints = jnp.concatenate([routes.T, ids[None, :]], axis=0)
    col_ints = jnp.concatenate([routes, ids[:, None]], axis=1)
    n_items = 4 * Z * E
    tab_rows = n_items + LANES
    H = max(Z // 2, 1)
    dma = pltpu.SemaphoreType.DMA
    vmem = pl.BlockSpec(memory_space=pltpu.VMEM)
    hbm = pl.BlockSpec(memory_space=pl.ANY)
    outs = pl.pallas_call(
        functools.partial(kernel, sizes),
        out_shape=(
            jax.ShapeDtypeStruct((8, LANES), f32),
            jax.ShapeDtypeStruct((LANES, FF), f32),
            jax.ShapeDtypeStruct((LANES, FF), f32),
            jax.ShapeDtypeStruct((FF, LANES), f32),
            jax.ShapeDtypeStruct((E, D), f32),
        ),
        in_specs=[
            hbm, pl.BlockSpec(memory_space=pltpu.SMEM), vmem, vmem, vmem, vmem, vmem,
            hbm, hbm, hbm, vmem,
        ],
        out_specs=(vmem,) * 5,
        scratch_shapes=[
            pltpu.VMEM((4, S, D), bf16),
            pltpu.VMEM((D, FF), bf16),
            pltpu.VMEM((D, FF), bf16),
            pltpu.VMEM((FF, D), bf16),
            pltpu.VMEM((tab_rows, D), bf16),
            pltpu.VMEM((Z * 2 * (D // LANES), LANES), f32),
            pltpu.VMEM((E * 2 * (D // LANES), LANES), f32),
            pltpu.VMEM((8, D), f32),
            pltpu.VMEM((S, LANES), i32),
            pltpu.VMEM((S, LANES), i32),
            pltpu.VMEM((S, 2 * R), bf16),
            pltpu.VMEM((2 * R, S), bf16),
            pltpu.VMEM((R, D), f32),
            pltpu.VMEM((R, D), bf16),
            pltpu.VMEM((8, D), f32),
            pltpu.VMEM((min(128, S), D), f32),
            pltpu.VMEM((S, D), bf16),
            pltpu.VMEM((D, S), bf16),
            pltpu.VMEM((S, FF), f32),
            pltpu.VMEM((S, FF), f32),
            pltpu.VMEM((S, FF), f32),
            pltpu.VMEM((S, FF), bf16),
            pltpu.VMEM((FF, S), bf16),
            pltpu.VMEM((2, S, FF), bf16),
            pltpu.VMEM((E, D), f32),
            pltpu.VMEM((E, E, D // E), f32),
            pltpu.VMEM((2 * Z, E, D // E), f32),
            pltpu.VMEM((E, E, D // E), f32),
            pltpu.VMEM((2, Z * LANES, FF), bf16),
            pltpu.VMEM((2, Z * LANES, FF), bf16),
            pltpu.VMEM((2, Z * LANES, FF), bf16),
            pltpu.VMEM((Z, FF, LANES), bf16),
            pltpu.VMEM((Z, FF, LANES), bf16),
            pltpu.VMEM((Z, FF, LANES), bf16),
            pltpu.VMEM((2, 2, H, LANES, FF), bf16),
            pltpu.VMEM((2, 2, H, FF // 2, LANES), bf16),
            dma((4,)), dma((4,)), dma((8,)), dma((8,)),
            dma((4, 2, H)), dma((4, 2, H)), dma((4, Z)), dma((4, Z)),
            dma((2, Z)), dma((2, Z)), dma((2, Z)), dma((2, Z)), dma((Z,)), dma((Z,)),
            dma((4, 2, H)), dma((4, 2, H)),
        ],
        compiler_params=pltpu.CompilerParams(
            collective_id=0, has_side_effects=True, vmem_limit_bytes=sizes["vmem"]
        ),
        cost_estimate=pl.CostEstimate(
            flops=7 * 2 * S * D * FF, bytes_accessed=2 * 4 * S * D, transcendentals=0
        ),
    )(
        history, lengths, user_query, pos_item, lane_ints, col_ints, w_router.T,
        w_gate, w_up, w_down, out_gain.reshape(1, D),
    )
    losses, grad_gate, grad_up, grad_down, grad_router = outs
    return losses[:2, 0], grad_gate[None], grad_up[None], grad_down[None], grad_router.T


def solution(mesh):
    both = ("dp", "expert")
    n_dp, n_expert = mesh.shape["dp"], mesh.shape["expert"]

    def whole(history, lengths, user_query, pos_item, neg_index, routes, w_router, w_gate, w_up, w_down, out_gain):
        rows = routes.shape[0] // (n_dp * n_expert)
        sizes = {
            "Z": n_dp // 2, "E": n_expert, "D": history.shape[2], "FF": w_gate.shape[2],
            "CAP": min(rows, 4 * rows // n_expert), "R": rows, "vmem": 63 << 20,
        }
        return jax.shard_map(
            functools.partial(local, sizes),
            mesh=mesh,
            in_specs=(
                P(both, None, None), P(both), P(both, None), P(both, None), P(both, None),
                P(both, None), P(), P("expert", "dp", None), P("expert", "dp", None),
                P("expert", None, "dp"), P(),
            ),
            out_specs=(
                P(both), P("expert", "dp", None), P("expert", "dp", None),
                P("expert", None, "dp"), P(),
            ),
            check_vma=False,
        )(history, lengths, user_query, pos_item, neg_index, routes, w_router, w_gate, w_up, w_down, out_gain)

    return whole
```

```python
import functools
import math

import jax
import jax.numpy as jnp
from jax import lax
from jax.experimental import pallas as pl
from jax.experimental.pallas import tpu as pltpu
from jax.sharding import PartitionSpec as P

HEAD = 128
CANDS = 64
EPS = 1e-6
LOSS_SCALE = 1024.0
LANES = 128

f32, bf16, i32 = jnp.float32, jnp.bfloat16, jnp.int32
NT = (((1,), (1,)), ((), ()))
TN = (((0,), (0,)), ((), ()))


def dot(a, b):
    return jnp.dot(a, b, preferred_element_type=f32)


def iota(shape, dim):
    return lax.broadcasted_iota(i32, shape, dim)


def kernel(
    sizes,
    hist, lens, q_ref, pos_ref, neg_ref, routes_ref, wr_ref, wg, wu, wd, gain_ref,
    loss_out, gg_out, gu_out, gd_out, gr_out,
    bufs, w_g, w_u, w_d, tab, pieces, ctx_pieces, ctx2, codes,
    s01, st, xh, nloc, gq_ref, xbuf, rows, rows_t, acc_g, acc_u, acc_h,
    hid, hid_t, d_gu, r_part, r_got, r_mid, r_fin,
    g_own, g_out, g_sib, d_own, d_out, d_sib, g_ring, d_ring,
    hist_sem, own_sem, small_s, small_r, ring_s, ring_r, sib_s, sib_r,
    a_s, a_r, gsib_s, gsib_r, dsib_s, dsib_r, sum_s, sum_r,
):
    Z, E, D, FF, CAP, R = (sizes[k] for k in ("Z", "E", "D", "FF", "CAP", "R"))
    S = E * CAP
    HEADS = D // HEAD
    PC = LANES
    NP = D // PC
    PR = 2 * NP
    FH = FF // 2
    N_ITEMS = 2 * E * 2 * Z
    HALF = N_ITEMS // 2
    BLK = 2 * Z
    TABW = tab.shape[0]
    CH = 2 * LANES

    dp = lax.axis_index("dp")
    me = lax.axis_index("expert")
    z = lax.div(dp, 2)
    c = lax.rem(dp, 2)
    sib_dp = 2 * z + 1 - c

    def at_z(off):
        return lax.rem(z + (off + Z), Z)

    def peer(j):
        if E == 16:
            x, y = lax.div(me, 4), lax.rem(me, 4)
            return lax.rem(x + lax.div(j, 4), 4) * 4 + lax.rem(y + lax.rem(j, 4), 4)
        return lax.rem(me + j, E)

    def mo(v, n):
        return pl.multiple_of(v, n)

    def remote(src, dst, s_sem, r_sem, to_dp, to_e):
        return pltpu.make_async_remote_copy(
            src_ref=src, dst_ref=dst, send_sem=s_sem, recv_sem=r_sem,
            device_id={"dp": to_dp, "expert": to_e},
            device_id_type=pl.DeviceIdType.MESH,
        )

    def took(ref, sem):
        pltpu.make_async_copy(ref, ref, sem).wait()

    def to_peers(make):
        @pl.loop(1, E)
        def _(j):
            make(peer(j)).start()

    drains = []

    hist_copies = [
        pltpu.make_async_copy(hist.at[n // 2, pl.ds((n % 2) * S, S), :], bufs.at[n], hist_sem.at[n])
        for n in range(4)
    ]
    own = (wg.at[0], wu.at[0], wd.at[0, pl.ds(0, FH), :], wd.at[0, pl.ds(FH, FH), :])

    def wref(t, of):
        if t < 2:
            return (w_g, w_u)[t].at[pl.ds(mo(of * LANES, LANES), LANES), :]
        return w_d.at[pl.ds((t - 2) * FH, FH), pl.ds(mo(of * LANES, LANES), LANES)]

    own_copies = [pltpu.make_async_copy(own[t], wref(t, dp), own_sem.at[t]) for t in range(4)]
    for cp in own_copies:
        cp.start()

    pos = pos_ref[...].astype(f32)
    for u in range(2):
        for j in range(NP):
            pieces[pl.ds(z * PR + NP * u + j, 1), :] = pos[u : u + 1, j * PC : (j + 1) * PC]

    barrier = pltpu.get_barrier_semaphore()

    @pl.loop(1, E)
    def _(j):
        pl.semaphore_signal(
            barrier, inc=1, device_id={"dp": dp, "expert": peer(j)},
            device_id_type=pl.DeviceIdType.MESH,
        )

    @pl.loop(1, 2 * Z)
    def _(j):
        pl.semaphore_signal(
            barrier, inc=1, device_id={"dp": lax.rem(dp + j, 2 * Z), "expert": me},
            device_id_type=pl.DeviceIdType.MESH,
        )

    pl.semaphore_wait(barrier, E - 1 + 2 * Z - 1)

    HOPS = [(Z // 2, Z // 2 - 1), (Z // 2 - 1, Z // 2)] * 2

    def ring_send(t, d, k, src, dst):
        cp = remote(
            src, dst, ring_s.at[t, d, k], ring_r.at[t, d, k],
            2 * at_z(1 if d == 0 else -1) + c, me,
        )
        cp.start()
        drains.append(cp.wait_send)

    def sib_send(t, idx, src, dst):
        cp = remote(src, dst, sib_s.at[t, idx], sib_r.at[t, idx], sib_dp, me)
        cp.start()
        drains.append(cp.wait_send)

    def ring_begin(types):
        for t in types:
            for d in range(2):
                if HOPS[t][d] > 0:
                    ring_send(t, d, 0, own[t], wref(t, dp))
        for t in types:
            sib_send(t, 0, own[t], wref(t, dp))

    def ring_event(types, k):
        for t in types:
            for d in range(2):
                if k > HOPS[t][d]:
                    continue
                off = -k if d == 0 else k
                r = wref(t, 2 * at_z(off) + c)
                took(r, ring_r.at[t, d, k - 1])
                if k < HOPS[t][d]:
                    ring_send(t, d, k, r, r)
                sib_send(t, off % Z, r, r)

    def sib_wait(types, off):
        for t in types:
            took(wref(t, 2 * at_z(off) + 1 - c), sib_r.at[t, off % Z])

    LAST = Z // 2
    events = [(t, k) for k in range(1, LAST + 1) for t in range(2)]

    def advance(until=None):
        while events:
            if until is not None and events[0][1] > until:
                return
            t, k = events.pop(0)
            ring_event((t,), k)
            if (t, k) == (1, LAST - 1):
                ring_begin((2, 3))
            if until is None:
                return

    my_piece = pieces.at[pl.ds(mo(z * PR, PR), PR), :]

    @pl.loop(1, Z)
    def _(k):
        remote(
            my_piece, my_piece, small_s.at[0], small_r.at[0],
            2 * lax.rem(z + k, Z) + c, me,
        ).start()

    drains.append(lambda: took(pieces.at[pl.ds(0, (Z - 1) * PR), :], small_s.at[0]))
    ring_begin((0, 1))
    for cp in hist_copies:
        cp.start()

    rt0, rt1 = routes_ref[0:1, :], routes_ref[1:2, :]
    row = iota((R, 1), 0)
    base = (dp * E + me) * 2
    id_f = jnp.where(row == 0, base, jnp.where(row == CANDS, base + 1, 0)).astype(f32)
    for u in range(2):
        at = iota((R, CANDS - 1), 0) == iota((R, CANDS - 1), 1) + (u * CANDS + 1)
        drawn = neg_ref[u : u + 1, :].astype(f32)
        id_f = id_f + jnp.sum(jnp.where(at, drawn, 0.0), axis=1, keepdims=True)
    diagonal = iota((R, R), 0) == iota((R, R), 1)
    id_col = id_f.astype(i32)
    id_lane = jnp.sum(jnp.where(diagonal, id_f, 0.0), axis=0, keepdims=True).astype(i32)

    def as_column(v):
        return jnp.sum(
            jnp.where(diagonal, v.astype(f32), 0.0), axis=1, keepdims=True
        ).astype(i32)

    def table_row(i):
        dev = lax.shift_right_logical(i, 1)
        of = lax.div(dev, E)
        return (
            lax.rem(of, 2) * HALF + lax.rem(dev, E) * BLK + lax.div(of, 2) * 2 + (i & 1)
        )

    e_sub = iota((E, R), 0)
    mt0, mt1 = e_sub == rt0, e_sub == rt1
    upper = (iota((R, R), 0) < iota((R, R), 1)).astype(bf16)
    rank_t = dot((mt0 | mt1).astype(bf16), upper) + (CAP * e_sub).astype(f32)
    slot0 = jnp.sum(jnp.where(mt0, rank_t, 0.0), axis=0, keepdims=True).astype(i32)
    slot1 = jnp.sum(jnp.where(mt1, rank_t, 0.0), axis=0, keepdims=True).astype(i32)
    s_sub = iota((S, R), 0)
    in0, in1 = s_sub == slot0, s_sub == slot1
    s01[:, 0:R] = in0.astype(bf16)
    s01[:, R : 2 * R] = in1.astype(bf16)
    my_slots = pl.ds(mo(me * CAP, CAP), CAP)
    r0, r1 = as_column(rt0), as_column(rt1)
    e_lane = iota((R, E), 1)
    m0, m1 = e_lane == r0, e_lane == r1
    lower = (iota((R, R), 1) < iota((R, R), 0)).astype(bf16)
    rank = dot(lower, (m0 | m1).astype(bf16)) + (CAP * e_lane).astype(f32)
    s_lane = iota((R, S), 1)
    user_col = me * 2 + (iota((R, 1), 0) >= CANDS).astype(i32)
    code_col = (table_row(id_col) + user_col * N_ITEMS + 1).astype(f32)
    code_row = jnp.full((1, S), -1.0, f32)
    for k, m in enumerate((m0, m1)):
        slot = jnp.sum(jnp.where(m, rank, 0.0), axis=1, keepdims=True).astype(i32)
        here = s_lane == slot
        st[k * R : (k + 1) * R, :] = here.astype(bf16)
        code_row = code_row + jnp.sum(jnp.where(here, code_col, 0.0), axis=0, keepdims=True)
    for n in range(S // LANES):
        codes[pl.ds(me * 8 + n, 1), :] = code_row[:, n * LANES : (n + 1) * LANES].astype(i32)
    my_codes = codes.at[pl.ds(mo(me * 8, 8), 8), :]
    all_codes = codes.at[pl.ds(0, (E - 1) * 8), :]
    to_peers(lambda p: remote(my_codes, my_codes, small_s.at[1], small_r.at[1], dp, p))
    drains.append(lambda: took(all_codes, small_s.at[1]))

    took(pieces.at[pl.ds(0, (Z - 1) * PR), :], small_r.at[0])
    my_block = pl.ds(mo(c * HALF + me * BLK, BLK), BLK)
    for j in range(NP):
        tab[my_block, j * PC : (j + 1) * PC] = pieces[pl.ds(j, BLK, stride=NP), :].astype(bf16)
    to_peers(
        lambda p: remote(
            tab.at[my_block, :], tab.at[my_block, :], small_s.at[2], small_r.at[2], dp, p
        )
    )
    drains.append(lambda: took(tab.at[pl.ds(0, (E - 1) * BLK), :], small_s.at[2]))

    in_head = lax.shift_right_logical(iota((HEADS, D), 1), 7) == iota((HEADS, D), 0)

    def attend(u):
        hist_copies[2 * u].wait()
        hist_copies[2 * u + 1].wait()
        qd = jnp.where(in_head, q_ref[u : u + 1, :].astype(f32), 0.0).astype(bf16)
        halves, tops = [], []
        for n in range(2):
            s = lax.dot_general(qd, bufs[2 * u + n], NT, preferred_element_type=f32)
            s = s * (1.0 / math.sqrt(HEAD))
            live = (iota((HEADS, S), 1) + n * S) < lens[u]
            s = jnp.where(live, s, -1e30)
            halves.append((s, live))
            tops.append(jnp.max(s, axis=1, keepdims=True))
        top = jnp.maximum(tops[0], tops[1])
        w = [jnp.where(live, jnp.exp(s - top), 0.0) for s, live in halves]
        total = jnp.sum(w[0], axis=1, keepdims=True) + jnp.sum(w[1], axis=1, keepdims=True)
        pooled = dot((w[0] / total).astype(bf16), bufs[2 * u]) + dot(
            (w[1] / total).astype(bf16), bufs[2 * u + 1]
        )
        ctx = jnp.sum(jnp.where(in_head, pooled, 0.0), axis=0, keepdims=True)
        ctx2[u : u + 1, :] = ctx
        for j in range(NP):
            ctx_pieces[pl.ds(me * PR + NP * u + j, 1), :] = ctx[:, j * PC : (j + 1) * PC]

    advance()
    attend(0)
    attend(1)
    my_ctx = ctx_pieces.at[pl.ds(mo(me * PR, PR), PR), :]
    to_peers(lambda p: remote(my_ctx, my_ctx, small_s.at[3], small_r.at[3], dp, p))
    drains.append(lambda: took(ctx_pieces.at[pl.ds(0, (E - 1) * PR), :], small_s.at[3]))
    for u in range(2):
        gq_ref[u : u + 1, :] = q_ref[u : u + 1, :].astype(f32) * gain_ref[...]
    for _ in range(3):
        advance()

    took(ctx_pieces.at[pl.ds(0, (E - 1) * PR), :], small_r.at[3])
    NU = 2 * E
    for j in range(NP):
        cols = slice(j * PC, (j + 1) * PC)
        v = ctx_pieces[pl.ds(j, NU, stride=NP), :]
        for n in range(3):
            part = v.astype(bf16)
            tab[N_ITEMS + n * NU : N_ITEMS + (n + 1) * NU, cols] = part
            v = v - part.astype(f32)
    tab[N_ITEMS + 3 * NU :, :] = jnp.zeros((TABW - N_ITEMS - 3 * NU, D), bf16)
    took(all_codes, small_r.at[1])

    took(tab.at[pl.ds(0, (E - 1) * BLK), :], small_r.at[2])
    my_half = tab.at[pl.ds(mo(c * HALF, HALF), HALF), :]
    half_copy = remote(my_half, my_half, small_s.at[4], small_r.at[4], sib_dp, me)
    half_copy.start()
    drains.append(half_copy.wait_send)
    advance()
    took(my_half, small_r.at[4])
    advance()

    NC = min(512, D)
    MT = min(128, S)

    def rebuild(m):
        here = pl.ds(mo(m * MT, MT), MT)
        PER = MT // CAP
        shift = lax.rem(me * CAP, LANES) if CAP < LANES else 0
        place = iota((CAP, LANES), 1) == iota((CAP, LANES), 0) + shift
        columns = []
        for n in range(PER):
            line = codes[pl.ds((m * PER + n) * 8 + lax.div(me * CAP, LANES), 1), :].astype(f32)
            columns.append(jnp.sum(jnp.where(place, line, 0.0), axis=1, keepdims=True))
        got = jnp.broadcast_to(jnp.concatenate(columns, axis=0).astype(i32), (MT, LANES))
        item = jnp.where(got >= 0, got & (N_ITEMS - 1), -1)
        user = lax.shift_right_arithmetic(got, N_ITEMS.bit_length() - 1)
        lane = iota((MT, LANES), 1)
        parts = [(item == lane + LANES * b).astype(bf16) for b in range(max(1, N_ITEMS // LANES))]
        if N_ITEMS < LANES:
            parts = [p[:, :N_ITEMS] for p in parts]
        parts.append(((user == lax.rem(lane, NU)) & (lane < 3 * NU)).astype(bf16))
        hot = jnp.concatenate(parts, axis=1)
        ss = jnp.zeros((MT, 1), f32)
        for n in range(D // NC):
            cols = slice(n * NC, (n + 1) * NC)
            x = dot(hot, tab[:, cols])
            xbuf[:, cols] = x
            ss = ss + jnp.sum(x * x, axis=1, keepdims=True)
        scale = lax.rsqrt(ss * (1.0 / D) + EPS)
        for n in range(D // NC):
            cols = slice(n * NC, (n + 1) * NC)
            y = (xbuf[:, cols] * scale).astype(bf16)
            rows[here, cols] = y
            rows_t[cols, here] = y.T

    pl.loop(0, S // MT)(rebuild)

    near_first = [0]
    for k in range(1, Z // 2):
        near_first += [k, -k]
    near_first.append(Z // 2)
    FT = 256

    def offs_at(k):
        if k == 0 or k == LAST:
            return [k]
        return [k, -k]

    own_copies[0].wait()
    own_copies[1].wait()
    for k in range(LAST + 1):
        advance(k)
        for off in offs_at(k):
            sib_wait((0, 1), off)
        parts = [pl.ds(mo(at_z(off) * CH, CH), CH) for off in offs_at(k)]
        @pl.loop(0, FF // FT)
        def _(n):
            f = pl.ds(mo(n * FT, FT), FT)
            for acc, w in ((acc_g, w_g), (acc_u, w_u)):
                v = dot(rows[:, parts[0]], w[parts[0], f])
                for cols in parts[1:]:
                    v = v + dot(rows[:, cols], w[cols, f])
                if k == 0:
                    acc[:, f] = v
                else:
                    acc[:, f] += v

    @pl.loop(0, S // 64)
    def _(m):
        here = pl.ds(mo(m * 64, 64), 64)
        g, up = acc_g[here, :], acc_u[here, :]
        sig = jax.nn.sigmoid(g)
        silu = g * sig
        hid[here, :] = (silu * up).astype(bf16)
        acc_g[here, :] = up * (sig * (1.0 + g * (1.0 - sig)))
        acc_u[here, :] = silu

    def exchange(way, i, cols, src, dst):
        to_peers(
            lambda p: remote(
                bufs.at[src, pl.ds(mo(p * CAP, CAP), CAP), cols], bufs.at[dst, my_slots, cols],
                a_s.at[way, i], a_r.at[way, i], dp, p,
            )
        )
        drains.append(lambda: took(bufs.at[src, pl.ds(0, S - CAP), cols], a_s.at[way, i]))

    done_k = 0
    for i, off in enumerate(near_first):
        if off == 0:
            own_copies[2].wait()
            own_copies[3].wait()
        if abs(off) > done_k:
            done_k = abs(off)
            ring_event((2, 3), done_k)
        sib_wait((2, 3), off)
        cols = pl.ds(mo(at_z(off) * CH, CH), CH)
        bufs[0, :, cols] = dot(hid[...], w_d[:, cols]).astype(bf16)
        bufs[1, my_slots, cols] = bufs[0, my_slots, cols]
        exchange(0, i, cols, 0, 1)

    for n in range(FF // LANES):
        f = slice(n * LANES, (n + 1) * LANES)
        hid_t[f, :] = hid[:, f].T

    first_user = iota((R, 1), 0) < CANDS

    def by_user(ref, cols):
        return jnp.where(first_user, ref[0:1, cols], ref[1:2, cols])

    oh = (iota((R, N_ITEMS), 1) == table_row(id_col)).astype(bf16)
    total = jnp.zeros((R, 1), f32)
    for n in range(D // NC):
        cols = slice(n * NC, (n + 1) * NC)
        x = dot(oh, tab[0:N_ITEMS, cols]) + by_user(ctx2, cols)
        xh[:, cols] = x
        total = total + jnp.sum(x * x, axis=1, keepdims=True)
    inv = lax.rsqrt(total * (1.0 / D) + EPS)
    for n in range(D // NC):
        cols = slice(n * NC, (n + 1) * NC)
        nloc[:, cols] = (xh[:, cols] * inv).astype(bf16)
    logits = lax.dot_general(nloc[...], wr_ref[...], NT, preferred_element_type=f32)
    affinity = jax.nn.sigmoid(logits)
    aff0 = jnp.sum(jnp.where(m0, affinity, 0.0), axis=1, keepdims=True)
    aff1 = jnp.sum(jnp.where(m1, affinity, 0.0), axis=1, keepdims=True)
    aff_total = aff0 + aff1
    mix0, mix1 = aff0 / aff_total, aff1 / aff_total

    sums = [jnp.zeros((R, 1), f32) for _ in range(6)]
    for i, off in enumerate(near_first):
        cols = pl.ds(mo(at_z(off) * CH, CH), CH)
        took(bufs.at[1, pl.ds(0, S - CAP), cols], a_r.at[0, i])
        e = dot(st[...], bufs[1, :, cols])
        e0, e1 = e[0:R], e[R : 2 * R]
        h = xh[:, cols] + mix0 * e0 + mix1 * e1
        xh[:, cols] = h
        gq = by_user(gq_ref, cols)
        terms = (h * h, h * gq, gq * e0, gq * e1, h * e0, h * e1)
        sums = [a + jnp.sum(t, axis=1, keepdims=True) for a, t in zip(sums, terms)]
    hh, hq, qe0, qe1, he0, he1 = sums

    inv_h = lax.rsqrt(hh * (1.0 / D) + EPS)
    listwise = hq * inv_h * (1.0 / math.sqrt(D))
    d_parts = []
    for u in range(2):
        lw = listwise[u * CANDS : (u + 1) * CANDS]
        top = jnp.max(lw, axis=0, keepdims=True)
        ex = jnp.exp(lw - top)
        ex_total = jnp.sum(ex, axis=0, keepdims=True)
        loss = jnp.log(ex_total) + top - lw[0:1]
        loss_out[u : u + 1, :] = jnp.broadcast_to(loss, (1, LANES))
        first = (iota((CANDS, 1), 0) == 0).astype(f32)
        d_parts.append(LOSS_SCALE * (ex / ex_total - first))
    d_list = jnp.concatenate(d_parts, axis=0) * (1.0 / math.sqrt(D))
    alpha = inv_h * d_list
    beta = alpha * inv_h * inv_h * hq * (1.0 / D)

    far_first = near_first[::-1]
    for i, off in enumerate(far_first):
        cols = pl.ds(mo(at_z(off) * CH, CH), CH)
        dh = alpha * by_user(gq_ref, cols) - beta * xh[:, cols]
        both = jnp.concatenate([(mix0 * dh).astype(bf16), (mix1 * dh).astype(bf16)], axis=0)
        bufs[2, :, cols] = dot(s01[...], both).astype(bf16)
        bufs[3, my_slots, cols] = bufs[2, my_slots, cols]
        exchange(1, i, cols, 2, 3)

    d_mix0, d_mix1 = alpha * qe0 - beta * he0, alpha * qe1 - beta * he1
    mix_dot = mix0 * d_mix0 + mix1 * d_mix1
    pick0 = (d_mix0 - mix_dot) / aff_total * aff0 * (1.0 - aff0)
    pick1 = (d_mix1 - mix_dot) / aff_total * aff1 * (1.0 - aff1)
    d_logits = (jnp.where(m0, pick0, 0.0) + jnp.where(m1, pick1, 0.0)).astype(bf16)
    DB = D // E
    r_part[...] = lax.dot_general(d_logits, nloc[...], TN, preferred_element_type=f32)
    my_cols = pl.ds(mo(me * DB, DB), DB)
    r_got[me] = r_part[:, my_cols]
    to_peers(
        lambda p: remote(
            r_part.at[:, pl.ds(mo(p * DB, DB), DB)], r_got.at[me],
            small_s.at[5], small_r.at[5], dp, p,
        )
    )
    drains.append(lambda: took(r_got.at[pl.ds(0, E - 1)], small_s.at[5]))

    def ring_slot(t, d, k):
        return g_ring.at[t, d, k] if t < 2 else d_ring.at[t - 2, d, k]

    def block(three, t, of):
        if t < 2:
            return three[0].at[t, pl.ds(mo(of * LANES, LANES), LANES), :]
        return three[1].at[of, pl.ds((t - 2) * FH, FH), :]

    mine = (g_own, d_own)
    theirs = (g_sib, d_sib)

    def add_rows(t, of, extra, out):
        height = LANES if t < 2 else FH
        step = 64

        @pl.loop(0, height // step)
        def _(m):
            here = pl.ds(mo(m * step, step), step)
            a, b = block(mine, t, of), block(theirs, t, of)
            v = a[here, :].astype(f32) + b[here, :].astype(f32)
            for r in extra:
                v = v + r[here, :].astype(f32)
            if out is None:
                a[here, :] = v.astype(bf16)
            else:
                out[here, :] = v

    def sum_send(t, d, k):
        of = at_z(k if d == 0 else -k)
        extra = []
        if k < HOPS[t][d]:
            r = ring_slot(t, d, k)
            took(r, sum_r.at[t, d, k])
            extra.append(r)
        add_rows(t, of, extra, None)
        cp = remote(
            block(mine, t, of), ring_slot(t, d, k - 1), sum_s.at[t, d, k - 1],
            sum_r.at[t, d, k - 1], 2 * at_z(1 if d == 0 else -1) + c, me,
        )
        cp.start()
        drains.append(cp.wait_send)

    def stage(types, n):
        first, second = types
        if n % 2:
            first, second = second, first
        k = LAST - (n + 1) // 2
        for t, d in ((first, 0), (second, 1)):
            sum_send(t, d, k)

    STAGES = 2 * LAST - 1

    def sum_last(t, out):
        extra = []
        for d in range(2):
            if HOPS[t][d] > 0:
                r = ring_slot(t, d, 0)
                took(r, sum_r.at[t, d, 0])
                extra.append(r)
        add_rows(t, z, extra, out)

    def down_wait(off):
        took(d_sib.at[at_z(off)], dsib_r.at[off % Z])

    def gate_wait(off):
        for t in range(2):
            took(block(theirs, t, at_z(off)), gsib_r.at[t, off % Z])

    def down_block(off):
        of = at_z(off)
        g = dot(hid_t[...], bufs[3, :, pl.ds(mo(of * CH, CH), CH)])
        low, high = g[:, :LANES], g[:, LANES:]
        d_out[of] = jnp.where(c == 0, high, low).astype(bf16)
        cp = remote(
            d_out.at[of], d_sib.at[of], dsib_s.at[off % Z], dsib_r.at[off % Z], sib_dp, me
        )
        cp.start()
        drains.append(cp.wait_send)
        d_own[of] = jnp.where(c == 0, low, high).astype(bf16)

    def down_pass(off):
        down_wait(off)
        k = abs(off)
        for t in (3, 2):
            for d in range(2):
                if k == LAST and HOPS[t][d] == LAST or k < LAST and d == (off < 0):
                    sum_send(t, d, k)

    i = 0
    for k in range(Z // 2, -1, -1):
        for off in reversed(offs_at(k)):
            of = at_z(off)
            cols = pl.ds(mo(of * CH, CH), CH)
            took(bufs.at[3, pl.ds(0, S - CAP), cols], a_r.at[1, i])
            got = bufs[3, :, cols]
            v = lax.dot_general(got, w_d[:, cols], NT, preferred_element_type=f32)
            if i == 0:
                acc_h[...] = v
            else:
                acc_h[...] += v
            if k > 0:
                down_block(off)
            if i > 0:
                down_pass(far_first[i - 1])
            i += 1

    @pl.loop(0, S // 64)
    def _(m):
        here = pl.ds(mo(m * 64, 64), 64)
        dh = acc_h[here, :]
        d_gu[0, here, :] = (dh * acc_g[here, :]).astype(bf16)
        d_gu[1, here, :] = (dh * acc_u[here, :]).astype(bf16)

    def gate_block(off):
        of = at_z(off)
        for core, dest in ((1 - c, g_out), (c, g_own)):
            at = pl.ds(mo((2 * of + core) * LANES, LANES), LANES)
            to = pl.ds(mo(of * LANES, LANES), LANES)
            for t in range(2):
                dest[t, to, :] = dot(rows_t[at, :], d_gu[t]).astype(bf16)
                if dest is g_out:
                    cp = remote(
                        block((g_out, d_out), t, of), block(theirs, t, of),
                        gsib_s.at[t, off % Z], gsib_r.at[t, off % Z], sib_dp, me,
                    )
                    cp.start()
                    drains.append(cp.wait_send)

    gate_block(LAST)
    gate_block(LAST - 1)
    gate_wait(LAST)
    stage((0, 1), 0)
    if LAST > 1:
        gate_block(1 - LAST)
    for off in offs_at(LAST - 1):
        gate_wait(off)
    if STAGES > 1:
        stage((0, 1), 1)
    down_block(0)

    took(r_got.at[pl.ds(0, E - 1)], small_r.at[5])
    part = r_got[0]
    for n in range(1, E):
        part = part + r_got[n]
    r_mid[dp] = part

    @pl.loop(1, 2 * Z)
    def _(j):
        remote(
            r_mid.at[dp], r_mid.at[dp], small_s.at[6], small_r.at[6],
            lax.rem(dp + j, 2 * Z), me,
        ).start()

    drains.append(lambda: took(r_mid.at[pl.ds(0, 2 * Z - 1)], small_s.at[6]))

    for k in range(LAST - 2, -1, -1):
        for off in offs_at(k):
            gate_block(off)
        for n in (2 * (LAST - k) - 2, 2 * (LAST - k) - 1):
            if n == 2 * (LAST - k) - 1:
                for off in offs_at(k):
                    gate_wait(off)
            if n < STAGES:
                stage((0, 1), n)

    down_wait(0)
    sum_last(2, gd_out.at[pl.ds(0, FH), :])
    sum_last(3, gd_out.at[pl.ds(FH, FH), :])

    took(r_mid.at[pl.ds(0, 2 * Z - 1)], small_r.at[6])
    part = r_mid[0]
    for n in range(1, 2 * Z):
        part = part + r_mid[n]
    r_fin[me] = part
    to_peers(
        lambda p: remote(r_fin.at[me], r_fin.at[me], small_s.at[7], small_r.at[7], dp, p)
    )
    drains.append(lambda: took(r_fin.at[pl.ds(0, E - 1)], small_s.at[7]))
    took(r_fin.at[pl.ds(0, E - 1)], small_r.at[7])
    for n in range(E):
        gr_out[:, n * DB : (n + 1) * DB] = r_fin[n]

    sum_last(0, gg_out)
    sum_last(1, gu_out)
    for drain in drains:
        drain()


def hand_out(loss, gg, gu, gd, gr, loss_out, gg_out, gu_out, gd_out, gr_out):
    gg_out[0] = gg[...]
    gu_out[0] = gu[...]
    gd_out[0] = gd[...]
    gr_out[...] = gr[...]
    for u in range(2):
        loss_out[u] = loss[u, 0]


def local(
    sizes, history, lengths, user_query, pos_item, neg_index, routes,
    w_router, w_gate, w_up, w_down, out_gain,
):
    Z, E, D, FF, CAP, R = (sizes[k] for k in ("Z", "E", "D", "FF", "CAP", "R"))
    S = E * CAP
    n_items = 4 * Z * E
    tab_rows = n_items + LANES
    H = max(Z // 2, 1)
    dma = pltpu.SemaphoreType.DMA
    vmem = pl.BlockSpec(memory_space=pltpu.VMEM)
    hbm = pl.BlockSpec(memory_space=pl.ANY)
    smem = pl.BlockSpec(memory_space=pltpu.SMEM)
    outs = pl.pallas_call(
        functools.partial(kernel, sizes),
        out_shape=(
            jax.ShapeDtypeStruct((8, LANES), f32),
            jax.ShapeDtypeStruct((LANES, FF), f32),
            jax.ShapeDtypeStruct((LANES, FF), f32),
            jax.ShapeDtypeStruct((FF, LANES), f32),
            jax.ShapeDtypeStruct((E, D), f32),
        ),
        in_specs=[
            hbm, smem, vmem, vmem, vmem, vmem, vmem,
            hbm, hbm, hbm, vmem,
        ],
        out_specs=(vmem,) * 5,
        scratch_shapes=[
            pltpu.VMEM((4, S, D), bf16),
            pltpu.VMEM((D, FF), bf16),
            pltpu.VMEM((D, FF), bf16),
            pltpu.VMEM((FF, D), bf16),
            pltpu.VMEM((tab_rows, D), bf16),
            pltpu.VMEM((Z * 2 * (D // LANES), LANES), f32),
            pltpu.VMEM((E * 2 * (D // LANES), LANES), f32),
            pltpu.VMEM((8, D), f32),
            pltpu.VMEM((E * 8, LANES), i32),
            pltpu.VMEM((S, 2 * R), bf16),
            pltpu.VMEM((2 * R, S), bf16),
            pltpu.VMEM((R, D), f32),
            pltpu.VMEM((R, D), bf16),
            pltpu.VMEM((8, D), f32),
            pltpu.VMEM((min(128, S), D), f32),
            pltpu.VMEM((S, D), bf16),
            pltpu.VMEM((D, S), bf16),
            pltpu.VMEM((S, FF), f32),
            pltpu.VMEM((S, FF), f32),
            pltpu.VMEM((S, FF), f32),
            pltpu.VMEM((S, FF), bf16),
            pltpu.VMEM((FF, S), bf16),
            pltpu.VMEM((2, S, FF), bf16),
            pltpu.VMEM((E, D), f32),
            pltpu.VMEM((E, E, D // E), f32),
            pltpu.VMEM((2 * Z, E, D // E), f32),
            pltpu.VMEM((E, E, D // E), f32),
            pltpu.VMEM((2, Z * LANES, FF), bf16),
            pltpu.VMEM((2, Z * LANES, FF), bf16),
            pltpu.VMEM((2, Z * LANES, FF), bf16),
            pltpu.VMEM((Z, FF, LANES), bf16),
            pltpu.VMEM((Z, FF, LANES), bf16),
            pltpu.VMEM((Z, FF, LANES), bf16),
            pltpu.VMEM((2, 2, H, LANES, FF), bf16),
            pltpu.VMEM((2, 2, H, FF // 2, LANES), bf16),
            dma((4,)), dma((4,)), dma((8,)), dma((8,)),
            dma((4, 2, H)), dma((4, 2, H)), dma((4, Z)), dma((4, Z)),
            dma((2, Z)), dma((2, Z)), dma((2, Z)), dma((2, Z)), dma((Z,)), dma((Z,)),
            dma((4, 2, H)), dma((4, 2, H)),
        ],
        compiler_params=pltpu.CompilerParams(
            collective_id=0, has_side_effects=True, vmem_limit_bytes=sizes["vmem"]
        ),
        cost_estimate=pl.CostEstimate(
            flops=7 * 2 * S * D * FF, bytes_accessed=2 * 4 * S * D, transcendentals=0
        ),
    )(
        history, lengths, user_query, pos_item, neg_index, routes.T, w_router.T,
        w_gate, w_up, w_down, out_gain.reshape(1, D),
    )
    losses, grad_gate, grad_up, grad_down, grad_router = pl.pallas_call(
        hand_out,
        out_shape=(
            jax.ShapeDtypeStruct((2,), f32),
            jax.ShapeDtypeStruct((1, LANES, FF), f32),
            jax.ShapeDtypeStruct((1, LANES, FF), f32),
            jax.ShapeDtypeStruct((1, FF, LANES), f32),
            jax.ShapeDtypeStruct((E, D), f32),
        ),
        in_specs=[smem, vmem, vmem, vmem, vmem],
        out_specs=(smem, vmem, vmem, vmem, vmem),
    )(*outs)
    return losses, grad_gate, grad_up, grad_down, grad_router.T


def solution(mesh):
    both = ("dp", "expert")
    n_dp, n_expert = mesh.shape["dp"], mesh.shape["expert"]

    def whole(history, lengths, user_query, pos_item, neg_index, routes, w_router, w_gate, w_up, w_down, out_gain):
        rows = routes.shape[0] // (n_dp * n_expert)
        sizes = {
            "Z": n_dp // 2, "E": n_expert, "D": history.shape[2], "FF": w_gate.shape[2],
            "CAP": min(rows, 4 * rows // n_expert), "R": rows, "vmem": 63 << 20,
        }
        return jax.shard_map(
            functools.partial(local, sizes),
            mesh=mesh,
            in_specs=(
                P(both, None, None), P(both), P(both, None), P(both, None), P(both, None),
                P(both, None), P(), P("expert", "dp", None), P("expert", "dp", None),
                P("expert", None, "dp"), P(),
            ),
            out_specs=(
                P(both), P("expert", "dp", None), P("expert", "dp", None),
                P("expert", None, "dp"), P(),
            ),
            check_vma=False,
        )(history, lengths, user_query, pos_item, neg_index, routes, w_router, w_gate, w_up, w_down, out_gain)

    return whole
```

```python
import functools
import math

import jax
import jax.numpy as jnp
from jax import lax
from jax.experimental import pallas as pl
from jax.experimental.pallas import tpu as pltpu
from jax.sharding import PartitionSpec as P

HEAD = 128
CANDS = 64
EPS = 1e-6
LOSS_SCALE = 1024.0
LANES = 128

f32, bf16, i32 = jnp.float32, jnp.bfloat16, jnp.int32
NT = (((1,), (1,)), ((), ()))
TN = (((0,), (0,)), ((), ()))


def dot(a, b):
    return jnp.dot(a, b, preferred_element_type=f32)


def iota(shape, dim):
    return lax.broadcasted_iota(i32, shape, dim)


def kernel(
    sizes,
    hist, lens, q_ref, pos_ref, neg_ref, routes_ref, wr_ref, wg, wu, wd, gain_ref,
    loss_out, gg_out, gu_out, gd_out, gr_out,
    bufs, w_g, w_u, w_d, tab, pieces, ctx_pieces, ctx2, codes,
    s01, st, xh, nloc, gq_ref, xbuf, rows, rows_t, acc_g, acc_u, acc_h,
    hid, hid_t, d_gu, r_part, r_got, r_mid, r_fin,
    g_own, g_out, g_sib, d_own, d_out, d_sib, g_ring, d_ring,
    hist_sem, own_sem, small_s, small_r, ring_s, ring_r, sib_s, sib_r,
    a_s, a_r, gsib_s, gsib_r, dsib_s, dsib_r, sum_s, sum_r,
):
    Z, E, D, FF, CAP, R = (sizes[k] for k in ("Z", "E", "D", "FF", "CAP", "R"))
    S = E * CAP
    HEADS = D // HEAD
    PC = LANES
    NP = D // PC
    PR = 2 * NP
    FH = FF // 2
    N_ITEMS = 2 * E * 2 * Z
    HALF = N_ITEMS // 2
    BLK = 2 * Z
    TABW = tab.shape[0]
    CH = 2 * LANES

    dp = lax.axis_index("dp")
    me = lax.axis_index("expert")
    z = lax.div(dp, 2)
    c = lax.rem(dp, 2)
    sib_dp = 2 * z + 1 - c

    def at_z(off):
        return lax.rem(z + (off + Z), Z)

    def peer(j):
        if E == 16:
            x, y = lax.div(me, 4), lax.rem(me, 4)
            return lax.rem(x + lax.div(j, 4), 4) * 4 + lax.rem(y + lax.rem(j, 4), 4)
        return lax.rem(me + j, E)

    def mo(v, n):
        return pl.multiple_of(v, n)

    def remote(src, dst, s_sem, r_sem, to_dp, to_e):
        return pltpu.make_async_remote_copy(
            src_ref=src, dst_ref=dst, send_sem=s_sem, recv_sem=r_sem,
            device_id={"dp": to_dp, "expert": to_e},
            device_id_type=pl.DeviceIdType.MESH,
        )

    def took(ref, sem):
        pltpu.make_async_copy(ref, ref, sem).wait()

    def to_peers(make):
        @pl.loop(1, E)
        def _(j):
            make(peer(j)).start()

    drains = []

    hist_copies = [
        pltpu.make_async_copy(hist.at[n // 2, pl.ds((n % 2) * S, S), :], bufs.at[n], hist_sem.at[n])
        for n in range(4)
    ]
    own = (wg.at[0], wu.at[0], wd.at[0, pl.ds(0, FH), :], wd.at[0, pl.ds(FH, FH), :])

    def wref(t, of):
        if t < 2:
            return (w_g, w_u)[t].at[pl.ds(mo(of * LANES, LANES), LANES), :]
        return w_d.at[pl.ds((t - 2) * FH, FH), pl.ds(mo(of * LANES, LANES), LANES)]

    own_copies = [pltpu.make_async_copy(own[t], wref(t, dp), own_sem.at[t]) for t in range(4)]
    for cp in own_copies:
        cp.start()

    pos = pos_ref[...].astype(f32)
    for u in range(2):
        for j in range(NP):
            pieces[pl.ds(z * PR + NP * u + j, 1), :] = pos[u : u + 1, j * PC : (j + 1) * PC]

    barrier = pltpu.get_barrier_semaphore()

    @pl.loop(1, E)
    def _(j):
        pl.semaphore_signal(
            barrier, inc=1, device_id={"dp": dp, "expert": peer(j)},
            device_id_type=pl.DeviceIdType.MESH,
        )

    @pl.loop(1, 2 * Z)
    def _(j):
        pl.semaphore_signal(
            barrier, inc=1, device_id={"dp": lax.rem(dp + j, 2 * Z), "expert": me},
            device_id_type=pl.DeviceIdType.MESH,
        )

    pl.semaphore_wait(barrier, E - 1 + 2 * Z - 1)

    HOPS = [(Z // 2, Z // 2 - 1), (Z // 2 - 1, Z // 2)] * 2

    def ring_send(t, d, k, src, dst):
        cp = remote(
            src, dst, ring_s.at[t, d, k], ring_r.at[t, d, k],
            2 * at_z(1 if d == 0 else -1) + c, me,
        )
        cp.start()
        drains.append(cp.wait_send)

    def sib_send(t, idx, src, dst):
        cp = remote(src, dst, sib_s.at[t, idx], sib_r.at[t, idx], sib_dp, me)
        cp.start()
        drains.append(cp.wait_send)

    def ring_begin(types):
        for t in types:
            for d in range(2):
                if HOPS[t][d] > 0:
                    ring_send(t, d, 0, own[t], wref(t, dp))
        for t in types:
            sib_send(t, 0, own[t], wref(t, dp))

    def ring_event(types, k):
        for t in types:
            for d in range(2):
                if k > HOPS[t][d]:
                    continue
                off = -k if d == 0 else k
                r = wref(t, 2 * at_z(off) + c)
                took(r, ring_r.at[t, d, k - 1])
                if k < HOPS[t][d]:
                    ring_send(t, d, k, r, r)
                sib_send(t, off % Z, r, r)

    def sib_wait(types, off):
        for t in types:
            took(wref(t, 2 * at_z(off) + 1 - c), sib_r.at[t, off % Z])

    LAST = Z // 2
    events = [(t, k) for k in range(1, LAST + 1) for t in range(2)]

    def advance(until=None):
        while events:
            if until is not None and events[0][1] > until:
                return
            t, k = events.pop(0)
            ring_event((t,), k)
            if (t, k) == (1, LAST - 1):
                ring_begin((2, 3))
            if until is None:
                return

    my_piece = pieces.at[pl.ds(mo(z * PR, PR), PR), :]

    @pl.loop(1, Z)
    def _(k):
        remote(
            my_piece, my_piece, small_s.at[0], small_r.at[0],
            2 * lax.rem(z + k, Z) + c, me,
        ).start()

    drains.append(lambda: took(pieces.at[pl.ds(0, (Z - 1) * PR), :], small_s.at[0]))
    ring_begin((0, 1))
    for cp in hist_copies:
        cp.start()

    took(pieces.at[pl.ds(0, (Z - 1) * PR), :], small_r.at[0])
    my_block = pl.ds(mo(c * HALF + me * BLK, BLK), BLK)
    for j in range(NP):
        tab[my_block, j * PC : (j + 1) * PC] = pieces[pl.ds(j, BLK, stride=NP), :].astype(bf16)
    to_peers(
        lambda p: remote(
            tab.at[my_block, :], tab.at[my_block, :], small_s.at[2], small_r.at[2], dp, p
        )
    )
    drains.append(lambda: took(tab.at[pl.ds(0, (E - 1) * BLK), :], small_s.at[2]))

    in_head = lax.shift_right_logical(iota((HEADS, D), 1), 7) == iota((HEADS, D), 0)

    def attend(u):
        hist_copies[2 * u].wait()
        hist_copies[2 * u + 1].wait()
        qd = jnp.where(in_head, q_ref[u : u + 1, :].astype(f32), 0.0).astype(bf16)
        halves, tops = [], []
        for n in range(2):
            s = lax.dot_general(qd, bufs[2 * u + n], NT, preferred_element_type=f32)
            s = s * (1.0 / math.sqrt(HEAD))
            live = (iota((HEADS, S), 1) + n * S) < lens[u]
            s = jnp.where(live, s, -1e30)
            halves.append((s, live))
            tops.append(jnp.max(s, axis=1, keepdims=True))
        top = jnp.maximum(tops[0], tops[1])
        w = [jnp.where(live, jnp.exp(s - top), 0.0) for s, live in halves]
        total = jnp.sum(w[0], axis=1, keepdims=True) + jnp.sum(w[1], axis=1, keepdims=True)
        pooled = dot((w[0] / total).astype(bf16), bufs[2 * u]) + dot(
            (w[1] / total).astype(bf16), bufs[2 * u + 1]
        )
        ctx = jnp.sum(jnp.where(in_head, pooled, 0.0), axis=0, keepdims=True)
        ctx2[u : u + 1, :] = ctx
        for j in range(NP):
            ctx_pieces[pl.ds(me * PR + NP * u + j, 1), :] = ctx[:, j * PC : (j + 1) * PC]

    attend(0)
    attend(1)
    my_ctx = ctx_pieces.at[pl.ds(mo(me * PR, PR), PR), :]
    to_peers(lambda p: remote(my_ctx, my_ctx, small_s.at[3], small_r.at[3], dp, p))
    drains.append(lambda: took(ctx_pieces.at[pl.ds(0, (E - 1) * PR), :], small_s.at[3]))
    for u in range(2):
        gq_ref[u : u + 1, :] = q_ref[u : u + 1, :].astype(f32) * gain_ref[...]
    advance()

    rt0, rt1 = routes_ref[0:1, :], routes_ref[1:2, :]
    row = iota((R, 1), 0)
    base = (dp * E + me) * 2
    id_f = jnp.where(row == 0, base, jnp.where(row == CANDS, base + 1, 0)).astype(f32)
    for u in range(2):
        at = iota((R, CANDS - 1), 0) == iota((R, CANDS - 1), 1) + (u * CANDS + 1)
        drawn = neg_ref[u : u + 1, :].astype(f32)
        id_f = id_f + jnp.sum(jnp.where(at, drawn, 0.0), axis=1, keepdims=True)
    diagonal = iota((R, R), 0) == iota((R, R), 1)
    id_col = id_f.astype(i32)
    id_lane = jnp.sum(jnp.where(diagonal, id_f, 0.0), axis=0, keepdims=True).astype(i32)

    def as_column(v):
        return jnp.sum(
            jnp.where(diagonal, v.astype(f32), 0.0), axis=1, keepdims=True
        ).astype(i32)

    def table_row(i):
        dev = lax.shift_right_logical(i, 1)
        of = lax.div(dev, E)
        return (
            lax.rem(of, 2) * HALF + lax.rem(dev, E) * BLK + lax.div(of, 2) * 2 + (i & 1)
        )

    e_sub = iota((E, R), 0)
    mt0, mt1 = e_sub == rt0, e_sub == rt1
    upper = (iota((R, R), 0) < iota((R, R), 1)).astype(bf16)
    rank_t = dot((mt0 | mt1).astype(bf16), upper) + (CAP * e_sub).astype(f32)
    slot0 = jnp.sum(jnp.where(mt0, rank_t, 0.0), axis=0, keepdims=True).astype(i32)
    slot1 = jnp.sum(jnp.where(mt1, rank_t, 0.0), axis=0, keepdims=True).astype(i32)
    s_sub = iota((S, R), 0)
    in0, in1 = s_sub == slot0, s_sub == slot1
    s01[:, 0:R] = in0.astype(bf16)
    s01[:, R : 2 * R] = in1.astype(bf16)
    my_slots = pl.ds(mo(me * CAP, CAP), CAP)
    r0, r1 = as_column(rt0), as_column(rt1)
    e_lane = iota((R, E), 1)
    m0, m1 = e_lane == r0, e_lane == r1
    lower = (iota((R, R), 1) < iota((R, R), 0)).astype(bf16)
    rank = dot(lower, (m0 | m1).astype(bf16)) + (CAP * e_lane).astype(f32)
    s_lane = iota((R, S), 1)
    user_col = me * 2 + (iota((R, 1), 0) >= CANDS).astype(i32)
    code_col = (table_row(id_col) + user_col * N_ITEMS + 1).astype(f32)
    code_row = jnp.full((1, S), -1.0, f32)
    for k, m in enumerate((m0, m1)):
        slot = jnp.sum(jnp.where(m, rank, 0.0), axis=1, keepdims=True).astype(i32)
        here = s_lane == slot
        st[k * R : (k + 1) * R, :] = here.astype(bf16)
        code_row = code_row + jnp.sum(jnp.where(here, code_col, 0.0), axis=0, keepdims=True)
    for n in range(S // LANES):
        codes[pl.ds(me * 8 + n, 1), :] = code_row[:, n * LANES : (n + 1) * LANES].astype(i32)
    my_codes = codes.at[pl.ds(mo(me * 8, 8), 8), :]
    all_codes = codes.at[pl.ds(0, (E - 1) * 8), :]
    to_peers(lambda p: remote(my_codes, my_codes, small_s.at[1], small_r.at[1], dp, p))
    drains.append(lambda: took(all_codes, small_s.at[1]))

    for _ in range(3):
        advance()

    took(ctx_pieces.at[pl.ds(0, (E - 1) * PR), :], small_r.at[3])
    NU = 2 * E
    for j in range(NP):
        cols = slice(j * PC, (j + 1) * PC)
        v = ctx_pieces[pl.ds(j, NU, stride=NP), :]
        for n in range(3):
            part = v.astype(bf16)
            tab[N_ITEMS + n * NU : N_ITEMS + (n + 1) * NU, cols] = part
            v = v - part.astype(f32)
    tab[N_ITEMS + 3 * NU :, :] = jnp.zeros((TABW - N_ITEMS - 3 * NU, D), bf16)
    took(all_codes, small_r.at[1])

    took(tab.at[pl.ds(0, (E - 1) * BLK), :], small_r.at[2])
    my_half = tab.at[pl.ds(mo(c * HALF, HALF), HALF), :]
    half_copy = remote(my_half, my_half, small_s.at[4], small_r.at[4], sib_dp, me)
    half_copy.start()
    drains.append(half_copy.wait_send)
    advance()
    took(my_half, small_r.at[4])
    advance()

    NC = min(512, D)
    MT = min(128, S)

    def rebuild(m):
        here = pl.ds(mo(m * MT, MT), MT)
        PER = MT // CAP
        shift = lax.rem(me * CAP, LANES) if CAP < LANES else 0
        place = iota((CAP, LANES), 1) == iota((CAP, LANES), 0) + shift
        columns = []
        for n in range(PER):
            line = codes[pl.ds((m * PER + n) * 8 + lax.div(me * CAP, LANES), 1), :].astype(f32)
            columns.append(jnp.sum(jnp.where(place, line, 0.0), axis=1, keepdims=True))
        got = jnp.broadcast_to(jnp.concatenate(columns, axis=0).astype(i32), (MT, LANES))
        item = jnp.where(got >= 0, got & (N_ITEMS - 1), -1)
        user = lax.shift_right_arithmetic(got, N_ITEMS.bit_length() - 1)
        lane = iota((MT, LANES), 1)
        parts = [(item == lane + LANES * b).astype(bf16) for b in range(max(1, N_ITEMS // LANES))]
        if N_ITEMS < LANES:
            parts = [p[:, :N_ITEMS] for p in parts]
        parts.append(((user == lax.rem(lane, NU)) & (lane < 3 * NU)).astype(bf16))
        hot = jnp.concatenate(parts, axis=1)
        ss = jnp.zeros((MT, 1), f32)
        for n in range(D // NC):
            cols = slice(n * NC, (n + 1) * NC)
            x = dot(hot, tab[:, cols])
            xbuf[:, cols] = x
            ss = ss + jnp.sum(x * x, axis=1, keepdims=True)
        scale = lax.rsqrt(ss * (1.0 / D) + EPS)
        for n in range(D // NC):
            cols = slice(n * NC, (n + 1) * NC)
            y = (xbuf[:, cols] * scale).astype(bf16)
            rows[here, cols] = y
            rows_t[cols, here] = y.T

    pl.loop(0, S // MT)(rebuild)

    near_first = [0]
    for k in range(1, Z // 2):
        near_first += [k, -k]
    near_first.append(Z // 2)
    FT = 256

    def offs_at(k):
        if k == 0 or k == LAST:
            return [k]
        return [k, -k]

    own_copies[0].wait()
    own_copies[1].wait()
    for k in range(LAST + 1):
        advance(k)
        for off in offs_at(k):
            sib_wait((0, 1), off)
        parts = [pl.ds(mo(at_z(off) * CH, CH), CH) for off in offs_at(k)]
        @pl.loop(0, FF // FT)
        def _(n):
            f = pl.ds(mo(n * FT, FT), FT)
            for acc, w in ((acc_g, w_g), (acc_u, w_u)):
                v = dot(rows[:, parts[0]], w[parts[0], f])
                for cols in parts[1:]:
                    v = v + dot(rows[:, cols], w[cols, f])
                if k == 0:
                    acc[:, f] = v
                else:
                    acc[:, f] += v

    @pl.loop(0, S // 64)
    def _(m):
        here = pl.ds(mo(m * 64, 64), 64)
        g, up = acc_g[here, :], acc_u[here, :]
        sig = jax.nn.sigmoid(g)
        silu = g * sig
        hid[here, :] = (silu * up).astype(bf16)
        acc_g[here, :] = up * (sig * (1.0 + g * (1.0 - sig)))
        acc_u[here, :] = silu

    def exchange(way, i, cols, src, dst):
        to_peers(
            lambda p: remote(
                bufs.at[src, pl.ds(mo(p * CAP, CAP), CAP), cols], bufs.at[dst, my_slots, cols],
                a_s.at[way, i], a_r.at[way, i], dp, p,
            )
        )
        drains.append(lambda: took(bufs.at[src, pl.ds(0, S - CAP), cols], a_s.at[way, i]))

    done_k = 0
    for i, off in enumerate(near_first):
        if off == 0:
            own_copies[2].wait()
            own_copies[3].wait()
        if abs(off) > done_k:
            done_k = abs(off)
            ring_event((2, 3), done_k)
        sib_wait((2, 3), off)
        cols = pl.ds(mo(at_z(off) * CH, CH), CH)
        bufs[0, :, cols] = dot(hid[...], w_d[:, cols]).astype(bf16)
        bufs[1, my_slots, cols] = bufs[0, my_slots, cols]
        exchange(0, i, cols, 0, 1)

    for n in range(FF // LANES):
        f = slice(n * LANES, (n + 1) * LANES)
        hid_t[f, :] = hid[:, f].T

    first_user = iota((R, 1), 0) < CANDS

    def by_user(ref, cols):
        return jnp.where(first_user, ref[0:1, cols], ref[1:2, cols])

    oh = (iota((R, N_ITEMS), 1) == table_row(id_col)).astype(bf16)
    total = jnp.zeros((R, 1), f32)
    for n in range(D // NC):
        cols = slice(n * NC, (n + 1) * NC)
        x = dot(oh, tab[0:N_ITEMS, cols]) + by_user(ctx2, cols)
        xh[:, cols] = x
        total = total + jnp.sum(x * x, axis=1, keepdims=True)
    inv = lax.rsqrt(total * (1.0 / D) + EPS)
    for n in range(D // NC):
        cols = slice(n * NC, (n + 1) * NC)
        nloc[:, cols] = (xh[:, cols] * inv).astype(bf16)
    logits = lax.dot_general(nloc[...], wr_ref[...], NT, preferred_element_type=f32)
    affinity = jax.nn.sigmoid(logits)
    aff0 = jnp.sum(jnp.where(m0, affinity, 0.0), axis=1, keepdims=True)
    aff1 = jnp.sum(jnp.where(m1, affinity, 0.0), axis=1, keepdims=True)
    aff_total = aff0 + aff1
    mix0, mix1 = aff0 / aff_total, aff1 / aff_total

    sums = [jnp.zeros((R, 1), f32) for _ in range(6)]
    for i, off in enumerate(near_first):
        cols = pl.ds(mo(at_z(off) * CH, CH), CH)
        took(bufs.at[1, pl.ds(0, S - CAP), cols], a_r.at[0, i])
        e = dot(st[...], bufs[1, :, cols])
        e0, e1 = e[0:R], e[R : 2 * R]
        h = xh[:, cols] + mix0 * e0 + mix1 * e1
        xh[:, cols] = h
        gq = by_user(gq_ref, cols)
        terms = (h * h, h * gq, gq * e0, gq * e1, h * e0, h * e1)
        sums = [a + jnp.sum(t, axis=1, keepdims=True) for a, t in zip(sums, terms)]
    hh, hq, qe0, qe1, he0, he1 = sums

    inv_h = lax.rsqrt(hh * (1.0 / D) + EPS)
    listwise = hq * inv_h * (1.0 / math.sqrt(D))
    d_parts = []
    for u in range(2):
        lw = listwise[u * CANDS : (u + 1) * CANDS]
        top = jnp.max(lw, axis=0, keepdims=True)
        ex = jnp.exp(lw - top)
        ex_total = jnp.sum(ex, axis=0, keepdims=True)
        loss = jnp.log(ex_total) + top - lw[0:1]
        loss_out[u : u + 1, :] = jnp.broadcast_to(loss, (1, LANES))
        first = (iota((CANDS, 1), 0) == 0).astype(f32)
        d_parts.append(LOSS_SCALE * (ex / ex_total - first))
    d_list = jnp.concatenate(d_parts, axis=0) * (1.0 / math.sqrt(D))
    alpha = inv_h * d_list
    beta = alpha * inv_h * inv_h * hq * (1.0 / D)

    far_first = near_first[::-1]
    for i, off in enumerate(far_first):
        cols = pl.ds(mo(at_z(off) * CH, CH), CH)
        dh = alpha * by_user(gq_ref, cols) - beta * xh[:, cols]
        both = jnp.concatenate([(mix0 * dh).astype(bf16), (mix1 * dh).astype(bf16)], axis=0)
        bufs[2, :, cols] = dot(s01[...], both).astype(bf16)
        bufs[3, my_slots, cols] = bufs[2, my_slots, cols]
        exchange(1, i, cols, 2, 3)

    d_mix0, d_mix1 = alpha * qe0 - beta * he0, alpha * qe1 - beta * he1
    mix_dot = mix0 * d_mix0 + mix1 * d_mix1
    pick0 = (d_mix0 - mix_dot) / aff_total * aff0 * (1.0 - aff0)
    pick1 = (d_mix1 - mix_dot) / aff_total * aff1 * (1.0 - aff1)
    d_logits = (jnp.where(m0, pick0, 0.0) + jnp.where(m1, pick1, 0.0)).astype(bf16)
    DB = D // E
    r_part[...] = lax.dot_general(d_logits, nloc[...], TN, preferred_element_type=f32)
    my_cols = pl.ds(mo(me * DB, DB), DB)
    r_got[me] = r_part[:, my_cols]
    to_peers(
        lambda p: remote(
            r_part.at[:, pl.ds(mo(p * DB, DB), DB)], r_got.at[me],
            small_s.at[5], small_r.at[5], dp, p,
        )
    )
    drains.append(lambda: took(r_got.at[pl.ds(0, E - 1)], small_s.at[5]))

    def ring_slot(t, d, k):
        return g_ring.at[t, d, k] if t < 2 else d_ring.at[t - 2, d, k]

    def block(three, t, of):
        if t < 2:
            return three[0].at[t, pl.ds(mo(of * LANES, LANES), LANES), :]
        return three[1].at[of, pl.ds((t - 2) * FH, FH), :]

    mine = (g_own, d_own)
    theirs = (g_sib, d_sib)

    def add_rows(t, of, extra, out):
        height = LANES if t < 2 else FH
        step = 64

        @pl.loop(0, height // step)
        def _(m):
            here = pl.ds(mo(m * step, step), step)
            a, b = block(mine, t, of), block(theirs, t, of)
            v = a[here, :].astype(f32) + b[here, :].astype(f32)
            for r in extra:
                v = v + r[here, :].astype(f32)
            if out is None:
                a[here, :] = v.astype(bf16)
            else:
                out[here, :] = v

    def sum_send(t, d, k):
        of = at_z(k if d == 0 else -k)
        extra = []
        if k < HOPS[t][d]:
            r = ring_slot(t, d, k)
            took(r, sum_r.at[t, d, k])
            extra.append(r)
        add_rows(t, of, extra, None)
        cp = remote(
            block(mine, t, of), ring_slot(t, d, k - 1), sum_s.at[t, d, k - 1],
            sum_r.at[t, d, k - 1], 2 * at_z(1 if d == 0 else -1) + c, me,
        )
        cp.start()
        drains.append(cp.wait_send)

    def stage(types, n):
        first, second = types
        if n % 2:
            first, second = second, first
        k = LAST - (n + 1) // 2
        for t, d in ((first, 0), (second, 1)):
            sum_send(t, d, k)

    STAGES = 2 * LAST - 1

    def sum_last(t, out):
        extra = []
        for d in range(2):
            if HOPS[t][d] > 0:
                r = ring_slot(t, d, 0)
                took(r, sum_r.at[t, d, 0])
                extra.append(r)
        add_rows(t, z, extra, out)

    def down_wait(off):
        took(d_sib.at[at_z(off)], dsib_r.at[off % Z])

    def gate_wait(off):
        for t in range(2):
            took(block(theirs, t, at_z(off)), gsib_r.at[t, off % Z])

    def down_block(off):
        of = at_z(off)
        g = dot(hid_t[...], bufs[3, :, pl.ds(mo(of * CH, CH), CH)])
        low, high = g[:, :LANES], g[:, LANES:]
        d_out[of] = jnp.where(c == 0, high, low).astype(bf16)
        cp = remote(
            d_out.at[of], d_sib.at[of], dsib_s.at[off % Z], dsib_r.at[off % Z], sib_dp, me
        )
        cp.start()
        drains.append(cp.wait_send)
        d_own[of] = jnp.where(c == 0, low, high).astype(bf16)

    def down_pass(off):
        down_wait(off)
        k = abs(off)
        for t in (3, 2):
            for d in range(2):
                if k == LAST and HOPS[t][d] == LAST or k < LAST and d == (off < 0):
                    sum_send(t, d, k)

    i = 0
    for k in range(Z // 2, -1, -1):
        for off in reversed(offs_at(k)):
            of = at_z(off)
            cols = pl.ds(mo(of * CH, CH), CH)
            took(bufs.at[3, pl.ds(0, S - CAP), cols], a_r.at[1, i])
            got = bufs[3, :, cols]
            v = lax.dot_general(got, w_d[:, cols], NT, preferred_element_type=f32)
            if i == 0:
                acc_h[...] = v
            else:
                acc_h[...] += v
            if k > 0:
                down_block(off)
            if i > 0:
                down_pass(far_first[i - 1])
            i += 1

    @pl.loop(0, S // 64)
    def _(m):
        here = pl.ds(mo(m * 64, 64), 64)
        dh = acc_h[here, :]
        d_gu[0, here, :] = (dh * acc_g[here, :]).astype(bf16)
        d_gu[1, here, :] = (dh * acc_u[here, :]).astype(bf16)

    def gate_block(off):
        of = at_z(off)
        for core, dest in ((1 - c, g_out), (c, g_own)):
            at = pl.ds(mo((2 * of + core) * LANES, LANES), LANES)
            to = pl.ds(mo(of * LANES, LANES), LANES)
            for t in range(2):
                dest[t, to, :] = dot(rows_t[at, :], d_gu[t]).astype(bf16)
                if dest is g_out:
                    cp = remote(
                        block((g_out, d_out), t, of), block(theirs, t, of),
                        gsib_s.at[t, off % Z], gsib_r.at[t, off % Z], sib_dp, me,
                    )
                    cp.start()
                    drains.append(cp.wait_send)

    gate_block(LAST)
    gate_block(LAST - 1)
    gate_wait(LAST)
    stage((0, 1), 0)
    if LAST > 1:
        gate_block(1 - LAST)
    for off in offs_at(LAST - 1):
        gate_wait(off)
    if STAGES > 1:
        stage((0, 1), 1)
    down_block(0)

    took(r_got.at[pl.ds(0, E - 1)], small_r.at[5])
    part = r_got[0]
    for n in range(1, E):
        part = part + r_got[n]
    r_mid[dp] = part

    @pl.loop(1, 2 * Z)
    def _(j):
        remote(
            r_mid.at[dp], r_mid.at[dp], small_s.at[6], small_r.at[6],
            lax.rem(dp + j, 2 * Z), me,
        ).start()

    drains.append(lambda: took(r_mid.at[pl.ds(0, 2 * Z - 1)], small_s.at[6]))

    for k in range(LAST - 2, -1, -1):
        for off in offs_at(k):
            gate_block(off)
        for n in (2 * (LAST - k) - 2, 2 * (LAST - k) - 1):
            if n == 2 * (LAST - k) - 1:
                for off in offs_at(k):
                    gate_wait(off)
            if n < STAGES:
                stage((0, 1), n)

    down_wait(0)
    sum_last(2, gd_out.at[pl.ds(0, FH), :])
    sum_last(3, gd_out.at[pl.ds(FH, FH), :])

    took(r_mid.at[pl.ds(0, 2 * Z - 1)], small_r.at[6])
    part = r_mid[0]
    for n in range(1, 2 * Z):
        part = part + r_mid[n]
    r_fin[me] = part
    to_peers(
        lambda p: remote(r_fin.at[me], r_fin.at[me], small_s.at[7], small_r.at[7], dp, p)
    )
    drains.append(lambda: took(r_fin.at[pl.ds(0, E - 1)], small_s.at[7]))
    took(r_fin.at[pl.ds(0, E - 1)], small_r.at[7])
    for n in range(E):
        gr_out[:, n * DB : (n + 1) * DB] = r_fin[n]

    sum_last(0, gg_out)
    sum_last(1, gu_out)
    for drain in drains:
        drain()


def hand_out(loss, gg, gu, gd, gr, loss_out, gg_out, gu_out, gd_out, gr_out):
    gg_out[0] = gg[...]
    gu_out[0] = gu[...]
    gd_out[0] = gd[...]
    gr_out[...] = gr[...]
    for u in range(2):
        loss_out[u] = loss[u, 0]


def local(
    sizes, history, lengths, user_query, pos_item, neg_index, routes,
    w_router, w_gate, w_up, w_down, out_gain,
):
    Z, E, D, FF, CAP, R = (sizes[k] for k in ("Z", "E", "D", "FF", "CAP", "R"))
    S = E * CAP
    n_items = 4 * Z * E
    tab_rows = n_items + LANES
    H = max(Z // 2, 1)
    dma = pltpu.SemaphoreType.DMA
    vmem = pl.BlockSpec(memory_space=pltpu.VMEM)
    hbm = pl.BlockSpec(memory_space=pl.ANY)
    smem = pl.BlockSpec(memory_space=pltpu.SMEM)
    outs = pl.pallas_call(
        functools.partial(kernel, sizes),
        out_shape=(
            jax.ShapeDtypeStruct((8, LANES), f32),
            jax.ShapeDtypeStruct((LANES, FF), f32),
            jax.ShapeDtypeStruct((LANES, FF), f32),
            jax.ShapeDtypeStruct((FF, LANES), f32),
            jax.ShapeDtypeStruct((E, D), f32),
        ),
        in_specs=[
            hbm, smem, vmem, vmem, vmem, vmem, vmem,
            hbm, hbm, hbm, vmem,
        ],
        out_specs=(vmem,) * 5,
        scratch_shapes=[
            pltpu.VMEM((4, S, D), bf16),
            pltpu.VMEM((D, FF), bf16),
            pltpu.VMEM((D, FF), bf16),
            pltpu.VMEM((FF, D), bf16),
            pltpu.VMEM((tab_rows, D), bf16),
            pltpu.VMEM((Z * 2 * (D // LANES), LANES), f32),
            pltpu.VMEM((E * 2 * (D // LANES), LANES), f32),
            pltpu.VMEM((8, D), f32),
            pltpu.VMEM((E * 8, LANES), i32),
            pltpu.VMEM((S, 2 * R), bf16),
            pltpu.VMEM((2 * R, S), bf16),
            pltpu.VMEM((R, D), f32),
            pltpu.VMEM((R, D), bf16),
            pltpu.VMEM((8, D), f32),
            pltpu.VMEM((min(128, S), D), f32),
            pltpu.VMEM((S, D), bf16),
            pltpu.VMEM((D, S), bf16),
            pltpu.VMEM((S, FF), f32),
            pltpu.VMEM((S, FF), f32),
            pltpu.VMEM((S, FF), f32),
            pltpu.VMEM((S, FF), bf16),
            pltpu.VMEM((FF, S), bf16),
            pltpu.VMEM((2, S, FF), bf16),
            pltpu.VMEM((E, D), f32),
            pltpu.VMEM((E, E, D // E), f32),
            pltpu.VMEM((2 * Z, E, D // E), f32),
            pltpu.VMEM((E, E, D // E), f32),
            pltpu.VMEM((2, Z * LANES, FF), bf16),
            pltpu.VMEM((2, Z * LANES, FF), bf16),
            pltpu.VMEM((2, Z * LANES, FF), bf16),
            pltpu.VMEM((Z, FF, LANES), bf16),
            pltpu.VMEM((Z, FF, LANES), bf16),
            pltpu.VMEM((Z, FF, LANES), bf16),
            pltpu.VMEM((2, 2, H, LANES, FF), bf16),
            pltpu.VMEM((2, 2, H, FF // 2, LANES), bf16),
            dma((4,)), dma((4,)), dma((8,)), dma((8,)),
            dma((4, 2, H)), dma((4, 2, H)), dma((4, Z)), dma((4, Z)),
            dma((2, Z)), dma((2, Z)), dma((2, Z)), dma((2, Z)), dma((Z,)), dma((Z,)),
            dma((4, 2, H)), dma((4, 2, H)),
        ],
        compiler_params=pltpu.CompilerParams(
            collective_id=0, has_side_effects=True, vmem_limit_bytes=sizes["vmem"]
        ),
        cost_estimate=pl.CostEstimate(
            flops=7 * 2 * S * D * FF, bytes_accessed=2 * 4 * S * D, transcendentals=0
        ),
    )(
        history, lengths, user_query, pos_item, neg_index, routes.T, w_router.T,
        w_gate, w_up, w_down, out_gain.reshape(1, D),
    )
    losses, grad_gate, grad_up, grad_down, grad_router = pl.pallas_call(
        hand_out,
        out_shape=(
            jax.ShapeDtypeStruct((2,), f32),
            jax.ShapeDtypeStruct((1, LANES, FF), f32),
            jax.ShapeDtypeStruct((1, LANES, FF), f32),
            jax.ShapeDtypeStruct((1, FF, LANES), f32),
            jax.ShapeDtypeStruct((E, D), f32),
        ),
        in_specs=[smem, vmem, vmem, vmem, vmem],
        out_specs=(smem, vmem, vmem, vmem, vmem),
    )(*outs)
    return losses, grad_gate, grad_up, grad_down, grad_router.T


def solution(mesh):
    both = ("dp", "expert")
    n_dp, n_expert = mesh.shape["dp"], mesh.shape["expert"]

    def whole(history, lengths, user_query, pos_item, neg_index, routes, w_router, w_gate, w_up, w_down, out_gain):
        rows = routes.shape[0] // (n_dp * n_expert)
        sizes = {
            "Z": n_dp // 2, "E": n_expert, "D": history.shape[2], "FF": w_gate.shape[2],
            "CAP": min(rows, 4 * rows // n_expert), "R": rows, "vmem": 63 << 20,
        }
        return jax.shard_map(
            functools.partial(local, sizes),
            mesh=mesh,
            in_specs=(
                P(both, None, None), P(both), P(both, None), P(both, None), P(both, None),
                P(both, None), P(), P("expert", "dp", None), P("expert", "dp", None),
                P("expert", None, "dp"), P(),
            ),
            out_specs=(
                P(both), P("expert", "dp", None), P("expert", "dp", None),
                P("expert", None, "dp"), P(),
            ),
            check_vma=False,
        )(history, lengths, user_query, pos_item, neg_index, routes, w_router, w_gate, w_up, w_down, out_gain)

    return whole
```
